128 devices in a mesh: head: 8 (over z, y_lo), exp: 16 (over y_hi, x, core).
Axes of the slice: x: 4, y: 4 (y_hi: 2, y_lo: 2; y = y_hi * 2 + y_lo), z: 4, core: 2. Of those that a mesh axis runs over, the one named last changes fastest.
Arguments:
- k_pre: bfloat16 [8, 32, 128, 4096], P(None, 'exp', None, 'head'), may hold values from -6 to 6
- v_pre: bfloat16 [8, 32, 128, 4096], P(None, 'exp', None, 'head'), may hold values from -6 to 6
- pre_decay: float32 [8, 32, 128, 32], P(None, 'exp', None, 'head'), may hold values from -1 to 0, as said below
- q_dec: bfloat16 [8, 32, 4, 4096], P('head', 'exp'), may hold values from -6 to 6
- k_dec: bfloat16 [8, 32, 4, 4096], P('head', 'exp'), may hold values from -6 to 6
- v_dec: bfloat16 [8, 32, 4, 4096], P('head', 'exp'), may hold values from -6 to 6
- dec_decay: float32 [8, 32, 4, 32], P('head', 'exp'), may hold values from -1 to 0, as said below
- x_dec: bfloat16 [8, 32, 4, 6144], P('head', 'exp'), may hold values from -6 to 6
- route: int32 [8, 32, 4, 2], P('head', 'exp'), may hold values from 0 to 15, all different within a row; in each aligned block of 8 rows (0 to 7, 8 to 15, ..., all dimensions but the last counted through in order) at most 2 rows name the same one
- att_gain: float32 [4096], replicated, may hold values from 0.25 to 1.75
- w_o: bfloat16 [4096, 6144], P('exp'), may hold values from -0.09375 to 0.09375
- ffn_gain: float32 [6144], replicated, may hold values from 0.25 to 1.75
- w_router: bfloat16 [6144, 16], replicated, may hold values from -0.15625 to 0.15625
- w_in: bfloat16 [16, 6144, 5120], P('exp', None, 'head'), may hold values from -0.078125 to 0.078125
- w_out: bfloat16 [16, 5120, 6144], P('exp', 'head'), may hold values from -0.078125 to 0.078125
Outputs:
- decoded: bfloat16 [8, 32, 4, 6144], P('head', 'exp')
The draws below stay inside these ranges and needn't reach their ends.
Inputs may be any that keep to these rules, and one draw needn't show every extreme that they name: `route`: each token names two different experts. In each aligned block of 8 tokens (the tokens of one device, in the order group, member, step) no expert is named by more than 2 tokens, a bound that some block reaches. `pre_decay`: log decay of a head at one token. `dec_decay`: log decay of a head at one step.
All inputs are finite; a program needn't handle non-finite values.
Results may differ from the reference program's by a relative error of at most 0.008.
Values may be sent and summed in bfloat16 or wider, within the bound.
No kernel may reach another device: no remote copies, remote signals or barrier semaphores. Data moves between devices by JAX's collectives and lax.ppermute only.
A program may use at most 128 MiB of HBM per device.

```python
import math
import jax
import jax.numpy as jnp
import numpy as np
from jax import lax

D = 6144
HEADS = 32
HD = 128
EXP_HID = 5120
CAP = 2
STEPS = 4
PREFILL = 128
REQ_DEV = 2
ATT = 4096
EXPERTS = 16
GROUPS = 8
OWNED = 32
N_HEAD = 8
N_EXP = 16


def decay_rates(key, low, high):
    base = jnp.exp(jax.random.uniform(jax.random.fold_in(key, 101), (HEADS,), jnp.float32, math.log(low), math.log(high)))
    factor = jnp.exp(jax.random.uniform(jax.random.fold_in(key, 102), (GROUPS, OWNED), jnp.float32, math.log(0.5), math.log(2.0)))
    return (base, factor)


def log_decay(key, base, factor, length, draw_probability):
    array_dimensions = (GROUPS, OWNED, length, HEADS)
    jitter = jax.random.uniform(jax.random.fold_in(key, 1), array_dimensions, jnp.float32, 0.5, 1.5)
    spike_factor = jax.random.uniform(jax.random.fold_in(key, 2), array_dimensions, jnp.float32) < draw_probability
    dropped_tokens = jnp.log(jax.random.uniform(jax.random.fold_in(key, 3), array_dimensions, jnp.float32, 0.5, 0.8))
    baseline_level = -base[None, None, None, :] * factor[:, :, None, None] * jitter
    return baseline_level + jnp.where(spike_factor, dropped_tokens, 0.0)


def draw_pre_decay(key, part):
    base, factor = decay_rates(key, 1.0 / 2000.0, 1.0 / 40.0)
    key = jax.random.fold_in(key, 11)
    return log_decay(key, base, factor, PREFILL, 2.0 / (PREFILL + STEPS))


def draw_dec_decay(key, part):
    base, factor = decay_rates(key, 1.0 / 2000.0, 1.0 / 40.0)
    key = jax.random.fold_in(key, 12)
    return log_decay(key, base, factor, STEPS, 2.0 / (PREFILL + STEPS))


def levels(rng, extent, pieces, least, high):
    level, own = 1.0, jax.random.fold_in(rng, 6)
    for axis_at, parts in pieces:
        steps = jnp.exp(jax.random.uniform(jax.random.fold_in(own, axis_at), (parts,), jnp.float32, least / len(pieces), high / len(pieces)))
        level = level * jnp.repeat(steps, extent[axis_at] // parts).reshape([-1 if axis == axis_at else 1 for axis in range(len(extent))])
    return level


def assign_block(stream_key, own, number, rows, count, top, bound, slope):
    ranking = jax.random.permutation(stream_key, count)
    heavy_load, ordinary = load_shares(count, rows * top, bound, slope, True), load_shares(count, rows * top, bound, slope, False)
    places = jnp.arange(count)

    def named(lengths, rotation):
        used = int((lengths > 0).sum())
        fixed = max(1, used // 4)
        moved = fixed + (places - fixed + rotation * (used - fixed)) % max(1, count - fixed)
        return jnp.zeros((count,), jnp.int32).at[ranking[jnp.where(places < fixed, places, moved)]].set(jnp.asarray(lengths, jnp.int32))

    lengths = jnp.where(number % 4 == 0, named(heavy_load, number // 4), named(ordinary, number - number // 4 - 1))
    mixed = jax.random.permutation(jax.random.fold_in(own, 3), count)
    donor, sink = mixed[0:count // 2 * 2:2], mixed[1:count // 2 * 2:2]
    margin = jnp.minimum(lengths[donor] - 1, bound - lengths[sink]) // 2
    margin = jnp.where((donor == ranking[0]) | (sink == ranking[0]) | (lengths[sink] == 0), 0, jnp.maximum(margin, 0))
    moved = jax.random.randint(jax.random.fold_in(own, 4), (count // 2,), 0, 1 << 20) % (margin + 1)
    lengths = lengths.at[donor].add(-moved).at[sink].add(moved)
    labels = jnp.searchsorted(jnp.cumsum(lengths), jnp.arange(rows * top), side="right").astype(jnp.int32)
    grid = labels.reshape(top, rows).T
    grid = grid[jax.random.permutation(jax.random.fold_in(own, 1), rows)]
    rotation = jax.random.randint(jax.random.fold_in(own, 2), (rows, 1), 0, top)
    return jnp.take_along_axis(grid, (jnp.arange(top)[None, :] + rotation) % top, axis=1)


def load_shares(count, total, limit, slope, full):
    weights = [(1 << 20) // math.isqrt(grade ** slope) + 1 for grade in range(1, count + 1)]
    largest = limit if full else min(limit, max(-(-total // count), total * weights[0] // sum(weights)))
    least = 1 if total - largest >= count - 1 else 0
    holding, rest = [largest] + [least] * (count - 1), total - largest - least * (count - 1)
    while rest > 0:
        movable = [i for i in range(1, count) if holding[i] < largest] or [i for i in range(1, count) if holding[i] < limit]
        whole, left = sum([weights[i] for i in movable]), rest
        for i in movable:
            addition = min(limit - holding[i], max(1, left * weights[i] // whole), rest)
            holding[i] = holding[i] + addition
            rest = rest - addition
    return np.array(holding)


def scatter_about(own_key, extent, deviation, most, shards=(), kind=jnp.bfloat16):
    array = deviation * jax.random.normal(own_key, extent, jnp.float32)
    if shards:
        array = array * levels(own_key, extent, shards, -0.22, 0.18)
    return jnp.clip(array, -most, most).astype(kind)


def setup_inputs(seed: int = 0) -> dict:
    key_of = jax.random.split(jax.random.key(seed), 16)
    k_pre = scatter_about(key_of[0], (GROUPS, OWNED, PREFILL, ATT), 1.0, 6.0, ((1, 16), (3, 8)))
    v_pre = scatter_about(key_of[1], (GROUPS, OWNED, PREFILL, ATT), 1.0, 6.0, ((1, 16), (3, 8)))
    pre_decay = draw_pre_decay(jax.random.fold_in(key_of[15], 71), 0)
    q_dec = scatter_about(key_of[3], (GROUPS, OWNED, STEPS, ATT), 1.0, 6.0, ((0, 8), (1, 16)))
    k_dec = scatter_about(key_of[4], (GROUPS, OWNED, STEPS, ATT), 1.0, 6.0, ((0, 8), (1, 16)))
    v_dec = scatter_about(key_of[5], (GROUPS, OWNED, STEPS, ATT), 1.0, 6.0, ((0, 8), (1, 16)))
    dec_decay = draw_dec_decay(jax.random.fold_in(key_of[15], 71), 0)
    x_dec = scatter_about(key_of[7], (GROUPS, OWNED, STEPS, D), 1.0, 6.0, ((0, 8), (1, 16)))
    route_keys = jax.random.split(jax.random.fold_in(key_of[8], 1), GROUPS * OWNED * STEPS // (REQ_DEV * STEPS))
    route_turns = jax.random.permutation(jax.random.fold_in(key_of[8], 3), GROUPS * OWNED * STEPS // (REQ_DEV * STEPS))
    route = jax.vmap(lambda own, number: assign_block(jax.random.fold_in(key_of[8], 2), own, number, REQ_DEV * STEPS, EXPERTS, 2, CAP, 1))(route_keys, route_turns).reshape((GROUPS, OWNED, STEPS, 2))
    att_gain = jnp.clip(1.0 + 0.15 * jax.random.normal(key_of[9], (ATT,), jnp.float32), 0.25, 1.75)
    w_o = scatter_about(key_of[10], (ATT, D), ATT ** -0.5, 0.09375, ((0, 16),))
    ffn_gain = jnp.clip(1.0 + 0.15 * jax.random.normal(key_of[11], (D,), jnp.float32), 0.25, 1.75)
    w_router = scatter_about(key_of[12], (D, EXPERTS), (D // 4) ** -0.5, 0.15625)
    w_in = scatter_about(key_of[13], (EXPERTS, D, EXP_HID), D ** -0.5, 0.078125, ((0, 16), (2, 8)))
    w_out = scatter_about(key_of[14], (EXPERTS, EXP_HID, D), EXP_HID ** -0.5, 0.078125, ((0, 16), (1, 8)))
    return {"k_pre": k_pre, "v_pre": v_pre, "pre_decay": pre_decay, "q_dec": q_dec, "k_dec": k_dec, "v_dec": v_dec, "dec_decay": dec_decay, "x_dec": x_dec, "route": route, "att_gain": att_gain, "w_o": w_o, "ffn_gain": ffn_gain, "w_router": w_router, "w_in": w_in, "w_out": w_out}


def rms_scale(values, gain):
    mean_square = lax.optimization_barrier(jnp.mean(values * values, axis=-1, keepdims=True))
    return values * lax.rsqrt(mean_square + 1e-06) * gain

def reference(k_pre, v_pre, pre_decay, q_dec, k_dec, v_dec, dec_decay, x_dec, route, att_gain, w_o, ffn_gain, w_router, w_in, w_out):
    highest = lax.Precision.HIGHEST
    cum = jnp.cumsum(pre_decay, axis=2)
    factor = jnp.exp(cum[:, :, -1:, :] - cum)
    split_shape = (GROUPS, OWNED, PREFILL, HEADS, HD)
    scaled_keys = (k_pre.reshape(split_shape).astype(jnp.float32) * factor[..., None]).astype(jnp.bfloat16)
    split_values = v_pre.reshape(split_shape)

    def one_group(items):
        keys_g, values_g, queries_d, keys_d, values_d, decay_d = items
        state = jnp.einsum('mlhd,mlhe->mhde', keys_g.astype(jnp.float32), values_g.astype(jnp.float32), precision=highest)
        readout_values = []
        for moment in range(STEPS):
            queries = queries_d[:, moment].reshape(OWNED, HEADS, HD).astype(jnp.float32)
            keys = keys_d[:, moment].reshape(OWNED, HEADS, HD).astype(jnp.float32)
            values = values_d[:, moment].reshape(OWNED, HEADS, HD).astype(jnp.float32)
            state = jnp.exp(decay_d[:, moment])[:, :, None, None] * state + keys[:, :, :, None] * values[:, :, None, :]
            readout = jnp.einsum('rhd,rhde->rhe', queries, state, precision=highest) / HD
            readout_values.append(readout.reshape(OWNED, ATT))
        return jnp.stack(readout_values, axis=1)
    readout = lax.map(one_group, (scaled_keys, split_values, q_dec, k_dec, v_dec, dec_decay))
    tokens = GROUPS * OWNED * STEPS
    normed = rms_scale(readout.reshape(tokens, ATT), att_gain).astype(jnp.bfloat16)
    attn = jnp.dot(normed, w_o, preferred_element_type=jnp.float32)
    resid = (x_dec.reshape(tokens, D).astype(jnp.float32) + attn).astype(jnp.bfloat16)
    resid_f = resid.astype(jnp.float32)
    ffn_in = rms_scale(resid_f, ffn_gain).astype(jnp.bfloat16)
    logits = jnp.dot(ffn_in, w_router, preferred_element_type=jnp.float32)
    expert_ids = route.reshape(tokens, 2)
    onehot = (expert_ids[:, :, None] == jnp.arange(EXPERTS, dtype=jnp.int32)[None, None, :]).astype(jnp.float32)
    picked_experts = lax.optimization_barrier(jnp.sum(onehot * logits[:, None, :], axis=-1))
    gates = jax.nn.sigmoid(picked_experts)
    weights = gates / lax.optimization_barrier(jnp.sum(gates, axis=-1, keepdims=True))
    devices = N_HEAD * N_EXP
    per_dev = 2 * REQ_DEV * STEPS
    block_ids = expert_ids.reshape(devices, per_dev)
    order = jnp.arange(per_dev, dtype=jnp.int32)
    earlier = (block_ids[:, :, None] == block_ids[:, None, :]) & (order[None, :, None] > order[None, None, :])
    slots = lax.optimization_barrier(jnp.sum(earlier.astype(jnp.int32), axis=-1))
    positions = (jnp.arange(devices, dtype=jnp.int32)[:, None] * CAP + slots).reshape(-1)
    flat_ids = block_ids.reshape(-1)
    assigns = devices * per_dev
    table = jnp.full((EXPERTS, devices * CAP), assigns, jnp.int32)
    table = table.at[flat_ids, positions].set(jnp.arange(assigns, dtype=jnp.int32))
    repeated = jnp.broadcast_to(ffn_in[:, None, :], (tokens, 2, D)).reshape(assigns, D)
    padded = jnp.concatenate([repeated, jnp.zeros((1, D), jnp.bfloat16)], axis=0)

    def run_expert(items):
        weight_in, weight_out, rows_index = items
        rows = padded[rows_index].astype(jnp.float32)
        hidden = jnp.dot(rows, weight_in.astype(jnp.float32), precision=highest)
        active = jax.nn.silu(hidden).astype(jnp.bfloat16)
        return jnp.dot(active.astype(jnp.float32), weight_out.astype(jnp.float32), precision=highest).astype(jnp.bfloat16)
    expert_out = lax.map(run_expert, (w_in, w_out, table))
    gathered = expert_out[flat_ids, positions].astype(jnp.float32).reshape(tokens, 2, D)
    decoded = resid_f + lax.optimization_barrier(jnp.sum(weights[:, :, None] * gathered, axis=1))
    return decoded.astype(jnp.bfloat16).reshape(GROUPS, OWNED, STEPS, D)
```

```python
import jax
import jax.numpy as jnp
from jax import lax
from jax.experimental import pallas as pl
from jax.experimental.pallas import tpu as pltpu
from jax.sharding import PartitionSpec as P

CAP = 2
EXTRA = 128
AXES = ("head", "exp")
F32 = jnp.float32
BF16 = jnp.bfloat16
HIGHEST = lax.Precision.HIGHEST


def device_pairs(move):
    pairs = []
    for head in range(8):
        for exp in range(16):
            to_head, to_exp = move(head, exp)
            pairs.append((head * 16 + exp, to_head * 16 + to_exp))
    return pairs


CORE = device_pairs(lambda head, exp: (head, exp ^ 1))
Y_LO = device_pairs(lambda head, exp: (head ^ 1, exp))
Z_UP = device_pairs(lambda head, exp: ((head + 2) % 8, exp))
Z_DOWN = device_pairs(lambda head, exp: ((head + 6) % 8, exp))
SWAP = device_pairs(lambda head, exp: (exp // 2, 2 * head + exp % 2))


def send(value, pairs):
    return lax.ppermute(value, AXES, pairs)


def split_two(value):
    high = lax.reduce_precision(value, 8, 7)
    return high.astype(BF16), (value - high).astype(BF16)


def split_three(value):
    high = lax.reduce_precision(value, 8, 7)
    rest = value - high
    middle = lax.reduce_precision(rest, 8, 7)
    return high.astype(BF16), middle.astype(BF16), (rest - middle).astype(BF16)


def readout_kernel(keys_ref, values_ref, decay_ref, dec_ref, gain_ref, out_ref):
    groups, members = keys_ref.shape[0], keys_ref.shape[1]
    heads = decay_ref.shape[2]
    length = decay_ref.shape[3]
    width = keys_ref.shape[3]
    head_dim = width // heads
    rows_per_head = dec_ref.shape[1] // 4
    steps = rows_per_head // members
    rows = heads * rows_per_head
    earlier = lax.broadcasted_iota(jnp.int32, (length, length), 0)
    later = lax.broadcasted_iota(jnp.int32, (length, length), 1)
    after = (earlier > later).astype(F32)
    row = lax.broadcasted_iota(jnp.int32, (rows, width), 0)
    lane = lax.broadcasted_iota(jnp.int32, (rows, width), 1)
    own_head = (row // rows_per_head) == (lane // head_dim)
    row_s = lax.broadcasted_iota(jnp.int32, (rows, length), 0)
    row_d = lax.broadcasted_iota(jnp.int32, (rows, rows_per_head), 0) % rows_per_head
    col_d = lax.broadcasted_iota(jnp.int32, (rows, rows_per_head), 1)
    causal = ((row_d // steps) == (col_d // steps)) & ((col_d % steps) <= (row_d % steps))
    extra_lane = lax.broadcasted_iota(jnp.int32, (rows_per_head, EXTRA), 1)
    results = []
    for group in range(groups):
        block = dec_ref[group].astype(F32)
        queries = block[0:rows_per_head]
        dec_keys = block[rows_per_head : 2 * rows_per_head]
        dec_values = block[2 * rows_per_head : 3 * rows_per_head]
        parts = block[3 * rows_per_head : 4 * rows_per_head]
        dec_cum = parts[:, 0:128] + parts[:, 128:256] + parts[:, 256:384]
        dec_cum = jnp.concatenate(
            [
                jnp.broadcast_to(dec_cum[:, h : h + 1], (rows_per_head, head_dim))
                for h in range(heads)
            ],
            axis=1,
        )
        spread = jnp.where(own_head, jnp.concatenate([queries] * heads, axis=0), 0.0).astype(BF16)
        total = jnp.zeros((rows, width), F32)
        for member in range(members):
            factor = jnp.exp(
                jnp.dot(
                    decay_ref[group, member], after, precision=HIGHEST, preferred_element_type=F32
                )
            )
            factor = jnp.concatenate(
                [jnp.broadcast_to(factor[h : h + 1], (rows_per_head, length)) for h in range(heads)],
                axis=0,
            )
            scores = lax.dot_general(
                spread,
                keys_ref[group, member],
                (((1,), (1,)), ((), ())),
                preferred_element_type=F32,
            )
            scores = jnp.where((row_s % rows_per_head) // steps == member, scores * factor, 0.0)
            high = scores.astype(BF16)
            low = (scores - high.astype(F32)).astype(BF16)
            both = jnp.dot(
                jnp.concatenate([high, low], axis=0),
                values_ref[group, member],
                preferred_element_type=F32,
            )
            total = total + both[:rows] + both[rows:]
        near = lax.dot_general(
            spread, dec_keys.astype(BF16), (((1,), (1,)), ((), ())), preferred_element_type=F32
        )
        near = jnp.where(causal, near, 0.0)
        total = total + jnp.dot(
            near, dec_values * jnp.exp(-dec_cum), precision=HIGHEST, preferred_element_type=F32
        )
        total = jnp.where(own_head, total, 0.0)
        readout = total[0:rows_per_head]
        for h in range(1, heads):
            readout = readout + total[h * rows_per_head : (h + 1) * rows_per_head]
        readout = readout * jnp.exp(dec_cum) * (1.0 / head_dim)
        squares = jnp.sum(readout * readout, axis=1, keepdims=True)
        high = squares.astype(BF16).astype(F32)
        extra = jnp.where(
            extra_lane == 0, high, jnp.where(extra_lane == 1, squares - high, 0.0)
        )
        results.append(jnp.concatenate([readout * gain_ref[...], extra], axis=1))
    out_ref[...] = jnp.concatenate(results, axis=0).astype(BF16)


def readout_features(k_pre, v_pre, decay, dec, gain):
    groups, members, length, width = k_pre.shape
    heads = decay.shape[2]
    rows_per_head = dec.shape[1] // 4
    batch = 2
    return pl.pallas_call(
        readout_kernel,
        grid=(groups // batch,),
        in_specs=[
            pl.BlockSpec((batch, members, length, width), lambda i: (i, 0, 0, 0)),
            pl.BlockSpec((batch, members, length, width), lambda i: (i, 0, 0, 0)),
            pl.BlockSpec((batch, members, heads, length), lambda i: (i, 0, 0, 0)),
            pl.BlockSpec((batch, 4 * rows_per_head, width), lambda i: (i, 0, 0)),
            pl.BlockSpec((1, width), lambda i: (0, 0)),
        ],
        out_specs=pl.BlockSpec((batch * rows_per_head, width + EXTRA), lambda i: (i, 0)),
        out_shape=jax.ShapeDtypeStruct((groups * rows_per_head, width + EXTRA), BF16),
        compiler_params=pltpu.CompilerParams(vmem_limit_bytes=32 << 20),
        cost_estimate=pl.CostEstimate(
            flops=2 * 2 * 64 * groups * members * length * width,
            bytes_accessed=4 * groups * members * length * width,
            transcendentals=0,
        ),
    )(k_pre, v_pre, decay, dec, gain)


def expert_kernel(rows_ref, order_ref, w_in_ref, w_out_ref, out_ref, hidden_ref, active_ref):
    step = pl.program_id(0)
    first = pl.num_programs(0) // 2

    @pl.when(step == 0)
    def _():
        hidden_ref[...] = jnp.zeros_like(hidden_ref)

    @pl.when(step < first)
    def _():
        hidden_ref[...] += jnp.dot(rows_ref[...], w_in_ref[...], preferred_element_type=F32)

    @pl.when(step == first - 1)
    def _():
        hidden = hidden_ref[...]
        active = (hidden * jax.nn.sigmoid(hidden)).astype(BF16)
        active_ref[...] = jnp.dot(
            order_ref[...], active, preferred_element_type=F32
        ).astype(BF16)

    @pl.when(step >= first)
    def _():
        out_ref[...] = jnp.dot(
            active_ref[...], w_out_ref[...], preferred_element_type=F32
        ).astype(BF16)


def run_expert(rows, order, w_in, w_out):
    count, model_dim = rows.shape
    hidden = w_in.shape[1]
    pieces = 4
    depth = model_dim // pieces
    return pl.pallas_call(
        expert_kernel,
        grid=(2 * pieces,),
        in_specs=[
            pl.BlockSpec((count, depth), lambda i: (0, jnp.minimum(i, pieces - 1))),
            pl.BlockSpec((count, count), lambda i: (0, 0)),
            pl.BlockSpec((depth, hidden), lambda i: (jnp.minimum(i, pieces - 1), 0)),
            pl.BlockSpec((hidden, depth), lambda i: (0, jnp.maximum(i - pieces, 0))),
        ],
        out_specs=pl.BlockSpec((count, depth), lambda i: (0, jnp.maximum(i - pieces, 0))),
        out_shape=jax.ShapeDtypeStruct((count, model_dim), BF16),
        scratch_shapes=[pltpu.VMEM((count, hidden), F32), pltpu.VMEM((count, hidden), BF16)],
        compiler_params=pltpu.CompilerParams(vmem_limit_bytes=40 << 20),
        cost_estimate=pl.CostEstimate(
            flops=4 * count * model_dim * hidden,
            bytes_accessed=4 * model_dim * hidden + 4 * count * model_dim,
            transcendentals=count * hidden,
        ),
    )(rows, order, w_in, w_out)


def gather_heads(own):
    half = own.shape[0] // 2
    from_down = send(own, Z_UP)
    from_up = send(own, Z_DOWN)
    beside = send(own, Y_LO)
    cross = send(jnp.concatenate([from_up[:half], from_down[:half]]), Y_LO)
    via_down = send(jnp.concatenate([from_down[:half], beside[half:]]), Z_UP)
    via_up = send(jnp.concatenate([from_up[half:], beside[half:]]), Z_DOWN)
    far = jnp.concatenate([via_down[:half], via_up[:half]])
    beside_up = jnp.concatenate([cross[:half], via_up[half:]])
    beside_down = jnp.concatenate([cross[half:], via_down[half:]])
    far_first = send(beside_down[:half], Z_UP)
    far_second = send(beside_up[half:], Z_DOWN)
    return jnp.concatenate(
        [own, from_up, from_down, far, beside, beside_up, beside_down, far_first, far_second]
    )


def add(first, *others):
    total = first.astype(F32)
    for other in others:
        total = total + other.astype(F32)
    return total.astype(BF16)


def scatter_heads(parts):
    own, up, down, far, beside, beside_up, beside_down, beside_far = parts
    half = own.shape[0] // 2
    first = send(beside_far[:half], Z_DOWN)
    second = send(beside_far[half:], Z_UP)
    beside_down_first = add(beside_down[:half], first)
    beside_up_second = add(beside_up[half:], second)
    cross = send(jnp.concatenate([beside_up[:half], beside_down_first]), Y_LO)
    to_down = send(jnp.concatenate([far[:half], beside_down[half:]]), Z_DOWN)
    to_up = send(jnp.concatenate([far[half:], beside_up_second]), Z_UP)
    up_sum = jnp.concatenate([add(up[:half], cross[:half]), add(up[half:], to_up[:half])])
    down_sum = jnp.concatenate([add(down[:half], cross[half:], to_down[:half]), down[half:]])
    beside_sum = jnp.concatenate([beside[:half], add(beside[half:], to_down[half:], to_up[half:])])
    from_beside = send(beside_sum, Y_LO)
    from_down = send(up_sum, Z_UP)
    from_up = send(down_sum, Z_DOWN)
    return add(own, from_beside, from_down, from_up)


def on_device(
    k_pre,
    v_pre,
    pre_decay,
    q_dec,
    k_dec,
    v_dec,
    dec_decay,
    x_dec,
    route,
    att_gain,
    w_o,
    ffn_gain,
    w_router,
    w_in,
    w_out,
):
    head_id, exp_id = lax.axis_index("head"), lax.axis_index("exp")
    core = exp_id % 2
    n_head, n_exp = lax.axis_size("head"), lax.axis_size("exp")
    local_heads = pre_decay.shape[3]
    owned, steps, width = q_dec.shape[1:]
    tokens = owned * steps
    model_dim = x_dec.shape[3]
    local_width = width // n_head

    w_o_other = send(w_o, CORE)
    ids = route.reshape(tokens, 2)
    carried = jnp.concatenate(
        [
            x_dec.reshape(tokens, model_dim),
            jnp.pad(ids.astype(BF16), ((0, 0), (0, EXTRA - 2))),
        ],
        axis=1,
    )
    carried = send(carried, SWAP)
    x_here = carried[:, :model_dim]
    ids_here = carried[:, model_dim : model_dim + 2].astype(jnp.int32)

    def by_head(array):
        split = array.reshape(tokens, n_head, local_width)
        return jnp.transpose(split, (1, 0, 2))

    cum = jnp.cumsum(dec_decay[0], axis=1).reshape(tokens, n_head, local_heads)
    cum = jnp.transpose(cum, (1, 0, 2))
    decay_rows = jnp.concatenate(
        [jnp.pad(part, ((0, 0), (0, 0), (0, 128 - local_heads))) for part in split_three(cum)],
        axis=2,
    )
    decay_rows = jnp.pad(decay_rows, ((0, 0), (0, 0), (0, local_width - 384)))
    packed = jnp.concatenate([by_head(q_dec), by_head(k_dec), by_head(v_dec), decay_rows], axis=1)
    packed = lax.all_to_all(packed, "head", split_axis=0, concat_axis=0, tiled=True)
    gain = lax.dynamic_slice(att_gain, (head_id * local_width,), (local_width,))
    features = readout_features(
        k_pre, v_pre, jnp.transpose(pre_decay, (0, 1, 3, 2)), packed, gain[None]
    )

    features = send(features, SWAP)
    half = local_width // 2
    mine = lax.dynamic_slice(features, (0, core * half), (features.shape[0], half))
    other = lax.dynamic_slice(features, (0, (1 - core) * half), (features.shape[0], half))
    partial_sum = jnp.dot(mine, w_o, preferred_element_type=F32) + jnp.dot(
        other, w_o_other, preferred_element_type=F32
    )
    partial_sum = jnp.concatenate(
        [partial_sum.astype(BF16), features[:, local_width:]], axis=1
    ).reshape(n_head, tokens, model_dim + EXTRA)
    parts = lax.all_to_all(
        partial_sum,
        "exp",
        split_axis=0,
        concat_axis=0,
        tiled=True,
        axis_index_groups=[list(range(c, n_exp, 2)) for c in range(2)],
    )
    summed = jnp.sum(parts.astype(F32), axis=0)
    squares = summed[:, model_dim : model_dim + 1] + summed[:, model_dim + 1 : model_dim + 2]
    attn = summed[:, :model_dim] * lax.rsqrt(squares / width + 1e-06)
    resid = (x_here.astype(F32) + attn).astype(BF16)
    resid_f = resid.astype(F32)
    mean_square = jnp.mean(resid_f * resid_f, axis=-1, keepdims=True)
    ffn_in = (resid_f * lax.rsqrt(mean_square + 1e-06) * ffn_gain).astype(BF16)

    experts = w_router.shape[1]
    logits = jnp.dot(ffn_in, w_router, preferred_element_type=F32)

    def slots_of(expert_ids):
        flat_ids = expert_ids.reshape(-1)
        order = jnp.arange(flat_ids.shape[0], dtype=jnp.int32)
        earlier = (flat_ids[:, None] == flat_ids[None, :]) & (order[:, None] > order[None, :])
        slots = jnp.sum(earlier.astype(jnp.int32), axis=1)
        target = (flat_ids * CAP + slots).reshape(tokens, 2)
        places = jnp.arange(experts * CAP, dtype=jnp.int32)
        return places[None, None, :] == target[:, :, None]

    table = jnp.sum(slots_of(ids_here).astype(F32), axis=1).astype(BF16)
    rows = jnp.dot(table.T, ffn_in, preferred_element_type=F32).astype(BF16)
    rows = rows.reshape(n_exp, CAP, model_dim)
    onehot = (ids_here[:, :, None] == jnp.arange(experts, dtype=jnp.int32)).astype(F32)
    gates = jax.nn.sigmoid(jnp.sum(onehot * logits[:, None, :], axis=-1))
    weights = gates / jnp.sum(gates, axis=-1, keepdims=True)
    weight_parts = jnp.concatenate(split_two(weights), axis=1)

    rows = lax.all_to_all(rows, "exp", split_axis=0, concat_axis=0, tiled=True)
    back = jnp.concatenate([resid, jnp.pad(weight_parts, ((0, 0), (0, EXTRA - 4)))], axis=1)
    back = send(back, SWAP)
    gathered = gather_heads(rows.reshape(n_exp * CAP, model_dim))

    count = gathered.shape[0]
    per_group = count // n_head // n_head
    offsets = jnp.array([0, 2, 6, 4, 1, 3, 7, 5], jnp.int32)

    def position(relative):
        step = offsets[relative]
        return ((head_id // 2 + step // 2) % 4) * 2 + (head_id % 2 + step % 2) % 2

    leaving = jnp.arange(count, dtype=jnp.int32)
    block = n_head * per_group
    goes_to = position(leaving // block)
    came_from = (leaving % block) // per_group
    key_out = (came_from * n_head + goes_to) * per_group + leaving % per_group
    key_in = (position(leaving // block) * n_head + (leaving % block) // per_group) * per_group
    key_in = key_in + leaving % per_group
    order = (key_out[:, None] == key_in[None, :]).astype(BF16)
    outputs = run_expert(gathered, order, w_in[0], w_out[0])
    outputs = scatter_heads([outputs[i * block : (i + 1) * block] for i in range(n_head)])
    returned = lax.all_to_all(
        outputs.reshape(n_exp, CAP, model_dim), "exp", split_axis=0, concat_axis=0, tiled=True
    ).reshape(n_exp * CAP, model_dim)

    weights_here = back[:, model_dim : model_dim + 2].astype(F32)
    weights_here = weights_here + back[:, model_dim + 2 : model_dim + 4].astype(F32)
    spread = jnp.sum(slots_of(ids).astype(F32) * weights_here[:, :, None], axis=1)
    mixed = jnp.dot(spread, returned.astype(F32), precision=HIGHEST)
    decoded = back[:, :model_dim].astype(F32) + mixed
    return decoded.astype(BF16).reshape(1, owned, steps, model_dim)


def solution(mesh):
    return jax.shard_map(
        on_device,
        mesh=mesh,
        in_specs=(
            P(None, "exp", None, "head"),
            P(None, "exp", None, "head"),
            P(None, "exp", None, "head"),
            P("head", "exp", None, None),
            P("head", "exp", None, None),
            P("head", "exp", None, None),
            P("head", "exp", None, None),
            P("head", "exp", None, None),
            P("head", "exp", None, None),
            P(),
            P("exp", None),
            P(),
            P(),
            P("exp", None, "head"),
            P("exp", "head", None),
        ),
        out_specs=P("head", "exp", None, None),
        check_vma=False,
    )
```

```python
import jax
import jax.numpy as jnp
from jax import lax
from jax.experimental import pallas as pl
from jax.experimental.pallas import tpu as pltpu
from jax.sharding import PartitionSpec as P

CAP = 2
EXTRA = 128
AXES = ("head", "exp")
F32 = jnp.float32
BF16 = jnp.bfloat16
HIGHEST = lax.Precision.HIGHEST


def device_pairs(move):
    pairs = []
    for head in range(8):
        for exp in range(16):
            to_head, to_exp = move(head, exp)
            pairs.append((head * 16 + exp, to_head * 16 + to_exp))
    return pairs


CORE = device_pairs(lambda head, exp: (head, exp ^ 1))
Y_LO = device_pairs(lambda head, exp: (head ^ 1, exp))
Z_UP = device_pairs(lambda head, exp: ((head + 2) % 8, exp))
Z_DOWN = device_pairs(lambda head, exp: ((head + 6) % 8, exp))
SWAP = device_pairs(lambda head, exp: (exp // 2, 2 * head + exp % 2))


def send(value, pairs):
    return lax.ppermute(value, AXES, pairs)


def split_two(value):
    high = lax.reduce_precision(value, 8, 7)
    return high.astype(BF16), (value - high).astype(BF16)


def whole(count):
    return [pl.BlockSpec(memory_space=pltpu.VMEM)] * count


def pack_kernel(
    queries_hbm,
    keys_hbm,
    values_hbm,
    decay_hbm,
    out_ref,
    queries_ref,
    keys_ref,
    values_ref,
    decay_ref,
    sems,
):
    sources = (queries_hbm, keys_hbm, values_hbm, decay_hbm)
    targets = (queries_ref, keys_ref, values_ref, decay_ref)
    copies = [
        pltpu.make_async_copy(source, target, sems.at[i])
        for i, (source, target) in enumerate(zip(sources, targets))
    ]
    for copy in copies:
        copy.start()
    for copy in copies:
        copy.wait()
    blocks, _, width = out_ref.shape
    members, steps = decay_ref.shape[1], decay_ref.shape[2]
    rows = []
    for member in range(members):
        running = decay_ref[0, member, 0:1]
        rows.append(running)
        for step in range(1, steps):
            running = running + decay_ref[0, member, step : step + 1]
            rows.append(running)
    summed = jnp.concatenate(rows, axis=0)
    count = members * steps
    heads = summed.shape[1]
    summed = jnp.concatenate([summed, jnp.zeros((count, 128 - heads), F32)], axis=1)
    high = summed.astype(BF16).astype(F32)
    rest = summed - high
    middle = rest.astype(BF16).astype(F32)
    pieces = [high, middle, rest - middle]
    if width > 384:
        pieces.append(jnp.zeros((count, width - 384), F32))
    decays = jnp.concatenate(pieces, axis=1)
    arrays = [
        jnp.concatenate([ref[0, m].astype(F32) for m in range(members)], axis=0)
        for ref in (queries_ref, keys_ref, values_ref)
    ]
    for block in range(blocks):
        lanes = slice(block * width, (block + 1) * width)
        out_ref[block] = jnp.concatenate(
            [array[:, lanes] for array in arrays] + [decays], axis=0
        ).astype(BF16)


def in_hbm(count):
    return [pl.BlockSpec(memory_space=pltpu.MemorySpace.HBM)] * count


def pin(*arrays):
    return [pltpu.with_memory_space_constraint(array, pltpu.MemorySpace.HBM) for array in arrays]


def pack_decode(q_dec, k_dec, v_dec, dec_decay, blocks):
    members, steps, width = q_dec.shape[1:]
    return pl.pallas_call(
        pack_kernel,
        in_specs=in_hbm(4),
        out_specs=whole(1)[0],
        out_shape=pltpu.HBM((blocks, 4 * members * steps, width // blocks), BF16),
        scratch_shapes=[pltpu.VMEM(array.shape, array.dtype) for array in (q_dec, k_dec, v_dec, dec_decay)]
        + [pltpu.SemaphoreType.DMA((4,))],
        compiler_params=pltpu.CompilerParams(vmem_limit_bytes=6 << 20),
    )(*pin(q_dec, k_dec, v_dec, dec_decay))


def readout_kernel(
    keys_hbm,
    values_hbm,
    decay_hbm,
    gain_hbm,
    dec_ref,
    out_ref,
    keys_ref,
    values_ref,
    decay_ref,
    gain_ref,
    sems,
):
    groups, members = keys_ref.shape[0], keys_ref.shape[1]
    heads = decay_ref.shape[2]
    length = decay_ref.shape[3]
    width = keys_ref.shape[3]
    head_dim = width // heads
    rows_per_head = dec_ref.shape[1] // 4
    steps = rows_per_head // members
    rows = heads * rows_per_head
    head_id = lax.axis_index("head")
    decay_copy = pltpu.make_async_copy(decay_hbm, decay_ref, sems.at[2 * groups])
    decay_copy.start()
    gain_copy = pltpu.make_async_copy(gain_hbm, gain_ref, sems.at[2 * groups + 1])
    gain_copy.start()
    copies = []
    for group in range(groups):
        copies.append(
            (
                pltpu.make_async_copy(keys_hbm.at[group], keys_ref.at[group], sems.at[group]),
                pltpu.make_async_copy(
                    values_hbm.at[group], values_ref.at[group], sems.at[groups + group]
                ),
            )
        )
        for copy in copies[-1]:
            copy.start()
    earlier = lax.broadcasted_iota(jnp.int32, (length, length), 0)
    later = lax.broadcasted_iota(jnp.int32, (length, length), 1)
    after = (earlier > later).astype(F32)
    row = lax.broadcasted_iota(jnp.int32, (rows, width), 0)
    lane = lax.broadcasted_iota(jnp.int32, (rows, width), 1)
    own_head = (row // rows_per_head) == (lane // head_dim)
    row_s = lax.broadcasted_iota(jnp.int32, (rows, length), 0)
    row_d = lax.broadcasted_iota(jnp.int32, (rows, rows_per_head), 0) % rows_per_head
    col_d = lax.broadcasted_iota(jnp.int32, (rows, rows_per_head), 1)
    causal = ((row_d // steps) == (col_d // steps)) & ((col_d % steps) <= (row_d % steps))
    extra_lane = lax.broadcasted_iota(jnp.int32, (rows_per_head, EXTRA), 1)
    decay_copy.wait()
    gain_copy.wait()
    gain = gain_ref[:, pl.ds(pl.multiple_of(head_id * width, width), width)]
    summed = jnp.concatenate(
        [decay_ref[g, m] for g in range(groups) for m in range(members)], axis=0
    )
    factors = jnp.exp(jnp.dot(summed, after, precision=HIGHEST, preferred_element_type=F32))

    half = groups // 2
    for start in (0, half):
        span = range(start, start + half)
        cums, spreads, blocks = {}, {}, {}
        for group in span:
            block = dec_ref[group].astype(F32)
            blocks[group] = block
            parts = block[3 * rows_per_head : 4 * rows_per_head]
            all_cum = parts[:, 0:128] + parts[:, 128:256] + parts[:, 256:384]
            cums[group] = jnp.concatenate(
                [
                    jnp.broadcast_to(
                        jnp.sum(
                            jnp.where(extra_lane == head_id * heads + h, all_cum, 0.0),
                            axis=1,
                            keepdims=True,
                        ),
                        (rows_per_head, head_dim),
                    )
                    for h in range(heads)
                ],
                axis=1,
            )
            queries = jnp.concatenate([block[0:rows_per_head]] * heads, axis=0)
            spreads[group] = jnp.where(own_head, queries, 0.0).astype(BF16)
        for group in span:
            for copy in copies[group]:
                copy.wait()
        pairs = [(group, member) for group in span for member in range(members)]
        scores = {
            (group, member): lax.dot_general(
                spreads[group],
                keys_ref[group, member],
                (((1,), (1,)), ((), ())),
                preferred_element_type=F32,
            )
            for group, member in pairs
        }
        near = {
            group: lax.dot_general(
                spreads[group],
                blocks[group][rows_per_head : 2 * rows_per_head].astype(BF16),
                (((1,), (1,)), ((), ())),
                preferred_element_type=F32,
            )
            for group in span
        }
        weighed = {}
        for group, member in pairs:
            first = (group * members + member) * heads
            factor = jnp.concatenate(
                [
                    jnp.broadcast_to(factors[first + h : first + h + 1], (rows_per_head, length))
                    for h in range(heads)
                ],
                axis=0,
            )
            score = scores[group, member] * factor
            score = jnp.where((row_s % rows_per_head) // steps == member, score, 0.0)
            high = score.astype(BF16)
            low = (score - high.astype(F32)).astype(BF16)
            weighed[group, member] = jnp.concatenate([high, low], axis=0)
        sums = {
            (group, member): jnp.dot(
                weighed[group, member], values_ref[group, member], preferred_element_type=F32
            )
            for group, member in pairs
        }
        results = []
        for group in span:
            cum = cums[group]
            values = blocks[group][2 * rows_per_head : 3 * rows_per_head] * jnp.exp(-cum)
            total = jnp.dot(
                jnp.where(causal, near[group], 0.0),
                values,
                precision=HIGHEST,
                preferred_element_type=F32,
            )
            for member in range(members):
                both = sums[group, member]
                total = total + both[:rows] + both[rows:]
            total = jnp.where(own_head, total, 0.0)
            readout = total[0:rows_per_head]
            for h in range(1, heads):
                readout = readout + total[h * rows_per_head : (h + 1) * rows_per_head]
            readout = readout * jnp.exp(cum) * (1.0 / head_dim)
            squares = jnp.sum(readout * readout, axis=1, keepdims=True)
            high = squares.astype(BF16).astype(F32)
            extra = jnp.where(
                extra_lane == 0, high, jnp.where(extra_lane == 1, squares - high, 0.0)
            )
            results.append(jnp.concatenate([readout * gain, extra], axis=1))
        at = slice(start * rows_per_head, (start + half) * rows_per_head)
        out_ref[at, :] = jnp.concatenate(results, axis=0).astype(BF16)


def readout_features(k_pre, v_pre, decay, dec, gain):
    groups, members, length, width = k_pre.shape
    count = groups * dec.shape[1] // 4
    return pl.pallas_call(
        readout_kernel,
        in_specs=in_hbm(4) + whole(1),
        out_specs=whole(1)[0],
        out_shape=jax.ShapeDtypeStruct((count, width + EXTRA), BF16),
        scratch_shapes=[
            pltpu.VMEM(k_pre.shape, BF16),
            pltpu.VMEM(v_pre.shape, BF16),
            pltpu.VMEM(decay.shape, F32),
            pltpu.VMEM(gain.shape, F32),
            pltpu.SemaphoreType.DMA((2 * groups + 2,)),
        ],
        compiler_params=pltpu.CompilerParams(vmem_limit_bytes=14 << 20),
        cost_estimate=pl.CostEstimate(
            flops=2 * 2 * 64 * groups * members * length * width,
            bytes_accessed=4 * groups * members * length * width,
            transcendentals=0,
        ),
    )(*pin(k_pre, v_pre, decay, gain), dec)


def stage_kernel(source_hbm, out_ref, sems):
    pieces = sems.shape[0]
    rows = out_ref.shape[0] // pieces
    copies = [
        pltpu.make_async_copy(
            source_hbm.at[pl.ds(i * rows, rows)], out_ref.at[pl.ds(i * rows, rows)], sems.at[i]
        )
        for i in range(pieces)
    ]
    for copy in copies:
        copy.start()
    for copy in copies:
        copy.wait()


def stage(weights):
    return pl.pallas_call(
        stage_kernel,
        in_specs=in_hbm(1),
        out_specs=whole(1)[0],
        out_shape=jax.ShapeDtypeStruct(weights.shape, weights.dtype),
        scratch_shapes=[pltpu.SemaphoreType.DMA((4,))],
        compiler_params=pltpu.CompilerParams(vmem_limit_bytes=2 << 20),
        cost_estimate=pl.CostEstimate(
            flops=0, bytes_accessed=2 * weights.size * 2, transcendentals=0
        ),
    )(*pin(weights))


def project_kernel(features_ref, own_ref, other_ref, out_ref):
    half, model_dim = own_ref.shape
    first = lax.axis_index("exp") % 2 == 0
    low, high = features_ref[:, 0:half], features_ref[:, half : 2 * half]
    mine = jnp.where(first, low, high)
    theirs = jnp.where(first, high, low)
    piece = model_dim // 2
    for at in (slice(0, piece), slice(piece, model_dim)):
        out_ref[:, at] = (
            jnp.dot(mine, own_ref[:, at], preferred_element_type=F32)
            + jnp.dot(theirs, other_ref[:, at], preferred_element_type=F32)
        ).astype(BF16)
    out_ref[:, model_dim:] = features_ref[:, 2 * half : 2 * half + EXTRA]


def project(features, own, other):
    count = features.shape[0]
    half, model_dim = own.shape
    return pl.pallas_call(
        project_kernel,
        in_specs=whole(3),
        out_specs=whole(1)[0],
        out_shape=jax.ShapeDtypeStruct((count, model_dim + EXTRA), BF16),
        compiler_params=pltpu.CompilerParams(vmem_limit_bytes=8 << 20),
        cost_estimate=pl.CostEstimate(
            flops=4 * count * half * model_dim,
            bytes_accessed=4 * half * model_dim,
            transcendentals=0,
        ),
    )(features, own, other)


def inward_kernel(rows_ref, w_in_ref, hidden_ref):
    depth = rows_ref.shape[1] // 2
    total = jnp.dot(rows_ref[:, :depth], w_in_ref[:depth, :], preferred_element_type=F32)
    hidden_ref[...] = total
    hidden_ref[...] += jnp.dot(rows_ref[:, depth:], w_in_ref[depth:, :], preferred_element_type=F32)


def inward(rows, w_in):
    count, model_dim = rows.shape
    hidden = w_in.shape[1]
    return pl.pallas_call(
        inward_kernel,
        in_specs=whole(2),
        out_specs=whole(1)[0],
        out_shape=pltpu.VMEM((count, hidden), F32),
        compiler_params=pltpu.CompilerParams(vmem_limit_bytes=6 << 20),
        cost_estimate=pl.CostEstimate(
            flops=2 * count * model_dim * hidden,
            bytes_accessed=2 * model_dim * hidden + 2 * count * model_dim,
            transcendentals=0,
        ),
    )(rows, w_in)


def middle_kernel(
    early_ref, rows_ref, order_ref, w_in_ref, w_out_hbm, active_ref, last_ref, w_out_ref, sems
):
    model_dim = rows_ref.shape[1]
    pieces = sems.shape[0]
    piece = model_dim // pieces
    copies = [
        pltpu.make_async_copy(
            w_out_hbm.at[:, pl.ds(i * piece, piece)],
            w_out_ref.at[:, pl.ds(i * piece, piece)],
            sems.at[i],
        )
        for i in range(pieces)
    ]
    for copy in copies:
        copy.start()
    late = jnp.dot(rows_ref[...], w_in_ref[...], preferred_element_type=F32)
    hidden = jnp.concatenate([early_ref[...], late], axis=0)
    active = (hidden * jax.nn.sigmoid(hidden)).astype(BF16)
    active = jnp.dot(order_ref[...], active, preferred_element_type=F32).astype(BF16)
    active_ref[...] = active
    last = active[early_ref.shape[0] :]
    for i, copy in enumerate(copies):
        copy.wait()
        at = slice(i * piece, (i + 1) * piece)
        last_ref[:, at] = jnp.dot(
            last, w_out_ref[:, at], preferred_element_type=F32
        ).astype(BF16)


def middle(early, rows, order, w_in, w_out):
    count, model_dim = rows.shape
    hidden = w_in.shape[1]
    total = early.shape[0] + count
    return pl.pallas_call(
        middle_kernel,
        in_specs=whole(4) + in_hbm(1),
        out_specs=whole(3),
        out_shape=[
            pltpu.VMEM((total, hidden), BF16),
            pltpu.VMEM((count, model_dim), BF16),
            pltpu.VMEM(w_out.shape, BF16),
        ],
        scratch_shapes=[pltpu.SemaphoreType.DMA((4,))],
        compiler_params=pltpu.CompilerParams(vmem_limit_bytes=8 << 20),
        cost_estimate=pl.CostEstimate(
            flops=4 * count * model_dim * hidden,
            bytes_accessed=4 * model_dim * hidden,
            transcendentals=total * hidden,
        ),
    )(early, rows, order, w_in, *pin(w_out))


def outward_kernel(active_ref, w_out_ref, out_ref):
    rows, model_dim = out_ref.shape
    piece = model_dim // 3
    active = active_ref[0:rows, :]
    for i in range(3):
        at = slice(i * piece, (i + 1) * piece)
        out_ref[:, at] = jnp.dot(
            active, w_out_ref[:, at], preferred_element_type=F32
        ).astype(BF16)


def outward(active, w_out, count):
    hidden, model_dim = w_out.shape
    return pl.pallas_call(
        outward_kernel,
        in_specs=whole(2),
        out_specs=whole(1)[0],
        out_shape=pltpu.VMEM((count, model_dim), BF16),
        compiler_params=pltpu.CompilerParams(vmem_limit_bytes=6 << 20),
        cost_estimate=pl.CostEstimate(
            flops=2 * count * model_dim * hidden,
            bytes_accessed=2 * model_dim * hidden + 2 * count * model_dim,
            transcendentals=0,
        ),
    )(active, w_out)


def gather_heads(own, weights, aside):
    half = own.shape[0] // 2
    from_down = send(own, Z_UP)
    from_up = send(own, Z_DOWN)
    beside = send(own, Y_LO)
    from_down, weights = lax.optimization_barrier((from_down, weights))
    cross = send(jnp.concatenate([from_up[:half], from_down[:half]]), Y_LO)
    via_down = send(jnp.concatenate([from_down[:half], beside[half:]]), Z_UP)
    via_up = send(jnp.concatenate([from_up[half:], beside[half:]]), Z_DOWN)
    far = jnp.concatenate([via_down[:half], via_up[:half]])
    beside_up = jnp.concatenate([cross[:half], via_up[half:]])
    beside_down = jnp.concatenate([cross[half:], via_down[half:]])
    far_first = send(beside_down[:half], Z_UP)
    far_second = send(beside_up[half:], Z_DOWN)
    weights = stage(weights)
    blocks = [own, from_up, from_down, far, beside, beside_up, beside_down]
    early = inward(jnp.concatenate(blocks), weights)
    aside, early = lax.optimization_barrier((aside, early))
    aside = send(aside, SWAP)
    return early, jnp.concatenate([far_first, far_second]), weights, aside


def add(first, *others):
    total = first.astype(F32)
    for other in others:
        total = total + other.astype(F32)
    return total.astype(BF16)


def gather_sums_kernel(parts_ref, cross_ref, down_ref, up_ref, to_up_ref, to_down_ref, beside_ref):
    rows = to_up_ref.shape[0]
    half = rows // 2
    low, high = slice(0, half), slice(half, rows)

    def part(block, which):
        return parts_ref[block * rows + which.start : block * rows + which.stop, :].astype(F32)

    cross = cross_ref[...].astype(F32)
    down = down_ref[...].astype(F32)
    up = up_ref[...].astype(F32)
    to_up_ref[low, :] = (part(1, low) + cross[low]).astype(BF16)
    to_up_ref[high, :] = (part(1, high) + up[low]).astype(BF16)
    to_down_ref[low, :] = (part(2, low) + cross[high] + down[low]).astype(BF16)
    to_down_ref[high, :] = parts_ref[2 * rows + half : 3 * rows, :]
    beside_ref[low, :] = parts_ref[4 * rows : 4 * rows + half, :]
    beside_ref[high, :] = (part(4, high) + down[high] + up[high]).astype(BF16)


def last_sum_kernel(parts_ref, first_ref, second_ref, third_ref, out_ref):
    rows = first_ref.shape[0]
    total = parts_ref[0:rows, :].astype(F32) + first_ref[...].astype(F32)
    total = total + second_ref[...].astype(F32) + third_ref[...].astype(F32)
    for i in range(out_ref.shape[0]):
        out_ref[i] = total[CAP * i : CAP * (i + 1)].astype(BF16)


def scatter_heads(parts, last):
    rows, width = last.shape
    half = rows // 2

    def block(i, start=0, stop=rows):
        return parts[i * rows + start : i * rows + stop]

    first = send(last[:half], Z_DOWN)
    second = send(last[half:], Z_UP)
    beside_down_first = add(block(6, 0, half), first)
    beside_up_second = add(block(5, half, rows), second)
    cross = send(jnp.concatenate([block(5, 0, half), beside_down_first]), Y_LO)
    to_down = send(jnp.concatenate([block(3, 0, half), block(6, half, rows)]), Z_DOWN)
    to_up = send(jnp.concatenate([block(3, half, rows), beside_up_second]), Z_UP)
    params = pltpu.CompilerParams(vmem_limit_bytes=6 << 20)
    cost = pl.CostEstimate(flops=0, bytes_accessed=12 * rows * width, transcendentals=0)
    up_sum, down_sum, beside_sum = pl.pallas_call(
        gather_sums_kernel,
        in_specs=whole(4),
        out_specs=whole(3),
        out_shape=[pltpu.VMEM((rows, width), BF16)] * 3,
        compiler_params=params,
        cost_estimate=cost,
    )(parts, cross, to_down, to_up)
    from_beside = send(beside_sum, Y_LO)
    from_down = send(up_sum, Z_UP)
    from_up = send(down_sum, Z_DOWN)
    return pl.pallas_call(
        last_sum_kernel,
        in_specs=whole(4),
        out_specs=whole(1)[0],
        out_shape=pltpu.HBM((rows // CAP, CAP, width), BF16),
        compiler_params=params,
        cost_estimate=cost,
    )(parts, from_beside, from_down, from_up)


def finish_kernel(returned_ref, resid_ref, weights_ref, out_ref):
    members, steps, width = out_ref.shape[1:]
    tokens = members * steps
    slots = weights_ref.shape[1]
    copies = returned_ref.shape[0] // slots
    piece = width // 4
    for i in range(4):
        at = slice(i * piece, (i + 1) * piece)
        total = returned_ref[0:slots, at].astype(F32)
        for copy in range(1, copies):
            total = total + returned_ref[copy * slots : (copy + 1) * slots, at].astype(F32)
        mixed = jnp.dot(weights_ref[...], total.astype(BF16), preferred_element_type=F32)
        mixed = mixed[:tokens] + mixed[tokens:]
        decoded = resid_ref[:, at].astype(F32) + mixed
        for member in range(members):
            out_ref[0, member, :, at] = decoded[member * steps : (member + 1) * steps].astype(BF16)


def finish(returned, resid, weights, members, steps, width):
    return pl.pallas_call(
        finish_kernel,
        in_specs=whole(3),
        out_specs=whole(1)[0],
        out_shape=jax.ShapeDtypeStruct((1, members, steps, width), BF16),
        compiler_params=pltpu.CompilerParams(vmem_limit_bytes=6 << 20),
    )(returned, resid, weights)


def on_device(
    k_pre,
    v_pre,
    pre_decay,
    q_dec,
    k_dec,
    v_dec,
    dec_decay,
    x_dec,
    route,
    att_gain,
    w_o,
    ffn_gain,
    w_router,
    w_in,
    w_out,
):
    head_id = lax.axis_index("head")
    n_head, n_exp = lax.axis_size("head"), lax.axis_size("exp")
    owned, steps, width = q_dec.shape[1:]
    tokens = owned * steps
    model_dim = x_dec.shape[3]

    w_o_other = send(w_o, CORE)

    packed = pack_decode(q_dec, k_dec, v_dec, dec_decay, n_head)
    packed = lax.all_to_all(packed, "head", split_axis=0, concat_axis=0, tiled=True)
    features = readout_features(
        k_pre, v_pre, jnp.transpose(pre_decay, (0, 1, 3, 2)), packed, att_gain[None]
    )

    ids = route.reshape(tokens, 2)
    carried = jnp.concatenate(
        [
            x_dec.reshape(tokens, model_dim),
            jnp.pad(ids.astype(BF16), ((0, 0), (0, EXTRA - 2))),
        ],
        axis=1,
    )
    features, carried = lax.optimization_barrier((features, carried))
    features = send(features, SWAP)
    carried = send(carried, SWAP)
    x_here = carried[:, :model_dim]
    ids_here = carried[:, model_dim : model_dim + 2].astype(jnp.int32)
    partial_sum = project(features, w_o, w_o_other)
    partial_sum = partial_sum.reshape(n_head, tokens, model_dim + EXTRA)
    parts = lax.all_to_all(
        partial_sum,
        "exp",
        split_axis=0,
        concat_axis=0,
        tiled=True,
        axis_index_groups=[list(range(c, n_exp, 2)) for c in range(2)],
    )
    summed = jnp.sum(parts.astype(F32), axis=0)
    squares = summed[:, model_dim : model_dim + 1] + summed[:, model_dim + 1 : model_dim + 2]
    attn = summed[:, :model_dim] * lax.rsqrt(squares / width + 1e-06)
    resid = (x_here.astype(F32) + attn).astype(BF16)
    resid_f = resid.astype(F32)
    mean_square = jnp.mean(resid_f * resid_f, axis=-1, keepdims=True)
    ffn_in = (resid_f * lax.rsqrt(mean_square + 1e-06) * ffn_gain).astype(BF16)

    experts = w_router.shape[1]
    logits = jnp.dot(ffn_in, w_router, preferred_element_type=F32)

    def slots_of(expert_ids):
        flat_ids = expert_ids.reshape(-1)
        order = jnp.arange(flat_ids.shape[0], dtype=jnp.int32)
        earlier = (flat_ids[:, None] == flat_ids[None, :]) & (order[:, None] > order[None, :])
        slots = jnp.sum(earlier.astype(jnp.int32), axis=1)
        target = (flat_ids * CAP + slots).reshape(tokens, 2)
        places = jnp.arange(experts * CAP, dtype=jnp.int32)
        return places[None, None, :] == target[:, :, None]

    table = jnp.sum(slots_of(ids_here).astype(F32), axis=1).astype(BF16)
    rows = jnp.dot(table.T, ffn_in, preferred_element_type=F32).astype(BF16)
    rows = rows.reshape(n_exp, CAP, model_dim)
    onehot = (ids_here[:, :, None] == jnp.arange(experts, dtype=jnp.int32)).astype(F32)
    gates = jax.nn.sigmoid(jnp.sum(onehot * logits[:, None, :], axis=-1))
    weights = gates / jnp.sum(gates, axis=-1, keepdims=True)
    weight_parts = jnp.concatenate(split_two(weights), axis=1)

    rows = lax.all_to_all(rows, "exp", split_axis=0, concat_axis=0, tiled=True)
    back = jnp.concatenate([resid, jnp.pad(weight_parts, ((0, 0), (0, EXTRA - 4)))], axis=1)
    early, late, near_in, back = gather_heads(
        rows.reshape(n_exp * CAP, model_dim), w_in[0], back
    )

    count = n_head * n_exp * CAP
    per_group = count // n_head // n_head
    offsets = jnp.array([0, 2, 6, 4, 1, 3, 7, 5], jnp.int32)

    def position(relative):
        step = offsets[relative]
        return ((head_id // 2 + step // 2) % 4) * 2 + (head_id % 2 + step % 2) % 2

    leaving = jnp.arange(count, dtype=jnp.int32)
    block = n_head * per_group
    goes_to = position(leaving // block)
    came_from = (leaving % block) // per_group
    key_out = (came_from * n_head + goes_to) * per_group + leaving % per_group
    key_in = (position(leaving // block) * n_head + (leaving % block) // per_group) * per_group
    key_in = key_in + leaving % per_group
    order = (key_out[:, None] == key_in[None, :]).astype(BF16)
    active, last, near_out = middle(early, late, order, near_in, w_out[0])
    last, back = lax.optimization_barrier((last, back))
    outputs = scatter_heads(outward(active, near_out, count - block), last)
    returned = lax.all_to_all(
        outputs, "exp", split_axis=0, concat_axis=0, tiled=True
    ).reshape(n_exp * CAP, model_dim)

    weights_here = back[:, model_dim : model_dim + 2].astype(F32)
    weights_here = weights_here + back[:, model_dim + 2 : model_dim + 4].astype(F32)
    spread = jnp.sum(slots_of(ids).astype(F32) * weights_here[:, :, None], axis=1)
    spread = jnp.concatenate(split_two(spread), axis=0)
    return finish(returned, back, spread, owned, steps, model_dim)


def solution(mesh):
    return jax.shard_map(
        on_device,
        mesh=mesh,
        in_specs=(
            P(None, "exp", None, "head"),
            P(None, "exp", None, "head"),
            P(None, "exp", None, "head"),
            P("head", "exp", None, None),
            P("head", "exp", None, None),
            P("head", "exp", None, None),
            P("head", "exp", None, None),
            P("head", "exp", None, None),
            P("head", "exp", None, None),
            P(),
            P("exp", None),
            P(),
            P(),
            P("exp", None, "head"),
            P("exp", "head", None),
        ),
        out_specs=P("head", "exp", None, None),
        check_vma=False,
    )
```

```python
import jax
import jax.numpy as jnp
from jax import lax
from jax.experimental import pallas as pl
from jax.experimental.pallas import tpu as pltpu
from jax.sharding import PartitionSpec as P

CAP = 2
EXTRA = 128
AXES = ("head", "exp")
F32 = jnp.float32
BF16 = jnp.bfloat16
HIGHEST = lax.Precision.HIGHEST


def device_pairs(move):
    pairs = []
    for head in range(8):
        for exp in range(16):
            to_head, to_exp = move(head, exp)
            pairs.append((head * 16 + exp, to_head * 16 + to_exp))
    return pairs


CORE = device_pairs(lambda head, exp: (head, exp ^ 1))
Y_LO = device_pairs(lambda head, exp: (head ^ 1, exp))
Z_UP = device_pairs(lambda head, exp: ((head + 2) % 8, exp))
Z_DOWN = device_pairs(lambda head, exp: ((head + 6) % 8, exp))
Z_FAR = device_pairs(lambda head, exp: ((head + 4) % 8, exp))
SWAP = device_pairs(lambda head, exp: (exp // 2, 2 * head + exp % 2))


def send(value, pairs):
    return lax.ppermute(value, AXES, pairs)


def split_two(value):
    high = lax.reduce_precision(value, 8, 7)
    return high.astype(BF16), (value - high).astype(BF16)


def whole(count):
    return [pl.BlockSpec(memory_space=pltpu.VMEM)] * count


def pack_kernel(
    queries_hbm,
    keys_hbm,
    values_hbm,
    decay_hbm,
    out_ref,
    queries_ref,
    keys_ref,
    values_ref,
    decay_ref,
    sems,
):
    sources = (queries_hbm, keys_hbm, values_hbm, decay_hbm)
    targets = (queries_ref, keys_ref, values_ref, decay_ref)
    copies = [
        pltpu.make_async_copy(source, target, sems.at[i])
        for i, (source, target) in enumerate(zip(sources, targets))
    ]
    for copy in copies:
        copy.start()
    for copy in copies:
        copy.wait()
    blocks, _, width = out_ref.shape
    members, steps = decay_ref.shape[1], decay_ref.shape[2]
    rows = []
    for member in range(members):
        running = decay_ref[0, member, 0:1]
        rows.append(running)
        for step in range(1, steps):
            running = running + decay_ref[0, member, step : step + 1]
            rows.append(running)
    summed = jnp.concatenate(rows, axis=0)
    count = members * steps
    heads = summed.shape[1]
    summed = jnp.concatenate([summed, jnp.zeros((count, 128 - heads), F32)], axis=1)
    high = summed.astype(BF16).astype(F32)
    rest = summed - high
    middle = rest.astype(BF16).astype(F32)
    pieces = [high, middle, rest - middle]
    if width > 384:
        pieces.append(jnp.zeros((count, width - 384), F32))
    decays = jnp.concatenate(pieces, axis=1)
    arrays = [
        jnp.concatenate([ref[0, m].astype(F32) for m in range(members)], axis=0)
        for ref in (queries_ref, keys_ref, values_ref)
    ]
    for block in range(blocks):
        lanes = slice(block * width, (block + 1) * width)
        out_ref[block] = jnp.concatenate(
            [array[:, lanes] for array in arrays] + [decays], axis=0
        ).astype(BF16)


def in_hbm(count):
    return [pl.BlockSpec(memory_space=pltpu.MemorySpace.HBM)] * count


def pin(*arrays):
    return [pltpu.with_memory_space_constraint(array, pltpu.MemorySpace.HBM) for array in arrays]


def pack_decode(q_dec, k_dec, v_dec, dec_decay, blocks):
    members, steps, width = q_dec.shape[1:]
    return pl.pallas_call(
        pack_kernel,
        in_specs=in_hbm(4),
        out_specs=whole(1)[0],
        out_shape=pltpu.HBM((blocks, 4 * members * steps, width // blocks), BF16),
        scratch_shapes=[pltpu.VMEM(array.shape, array.dtype) for array in (q_dec, k_dec, v_dec, dec_decay)]
        + [pltpu.SemaphoreType.DMA((4,))],
        compiler_params=pltpu.CompilerParams(vmem_limit_bytes=6 << 20),
    )(*pin(q_dec, k_dec, v_dec, dec_decay))


def readout_kernel(
    keys_hbm,
    values_hbm,
    decay_hbm,
    gain_hbm,
    dec_ref,
    out_ref,
    keys_ref,
    values_ref,
    decay_ref,
    gain_ref,
    sems,
):
    groups, members = keys_ref.shape[0], keys_ref.shape[1]
    heads = decay_ref.shape[2]
    length = decay_ref.shape[3]
    width = keys_ref.shape[3]
    head_dim = width // heads
    rows_per_head = dec_ref.shape[1] // 4
    steps = rows_per_head // members
    rows = heads * rows_per_head
    head_id = lax.axis_index("head")
    decay_copy = pltpu.make_async_copy(decay_hbm, decay_ref, sems.at[2 * groups])
    decay_copy.start()
    gain_copy = pltpu.make_async_copy(gain_hbm, gain_ref, sems.at[2 * groups + 1])
    gain_copy.start()
    copies = []
    for group in range(groups):
        copies.append(
            (
                pltpu.make_async_copy(keys_hbm.at[group], keys_ref.at[group], sems.at[group]),
                pltpu.make_async_copy(
                    values_hbm.at[group], values_ref.at[group], sems.at[groups + group]
                ),
            )
        )
        for copy in copies[-1]:
            copy.start()
    earlier = lax.broadcasted_iota(jnp.int32, (length, length), 0)
    later = lax.broadcasted_iota(jnp.int32, (length, length), 1)
    after = (earlier > later).astype(F32)
    row = lax.broadcasted_iota(jnp.int32, (rows, width), 0)
    lane = lax.broadcasted_iota(jnp.int32, (rows, width), 1)
    own_head = (row // rows_per_head) == (lane // head_dim)
    row_s = lax.broadcasted_iota(jnp.int32, (rows, length), 0)
    row_d = lax.broadcasted_iota(jnp.int32, (rows, rows_per_head), 0) % rows_per_head
    col_d = lax.broadcasted_iota(jnp.int32, (rows, rows_per_head), 1)
    causal = ((row_d // steps) == (col_d // steps)) & ((col_d % steps) <= (row_d % steps))
    extra_lane = lax.broadcasted_iota(jnp.int32, (rows_per_head, EXTRA), 1)
    decay_copy.wait()
    gain_copy.wait()
    gain = gain_ref[:, pl.ds(pl.multiple_of(head_id * width, width), width)]
    summed = jnp.concatenate(
        [decay_ref[g, m] for g in range(groups) for m in range(members)], axis=0
    )
    factors = jnp.exp(jnp.dot(summed, after, precision=HIGHEST, preferred_element_type=F32))

    half = groups // 2
    for start in (0, half):
        span = range(start, start + half)
        cums, spreads, blocks = {}, {}, {}
        for group in span:
            block = dec_ref[group].astype(F32)
            blocks[group] = block
            parts = block[3 * rows_per_head : 4 * rows_per_head]
            all_cum = parts[:, 0:128] + parts[:, 128:256] + parts[:, 256:384]
            cums[group] = jnp.concatenate(
                [
                    jnp.broadcast_to(
                        jnp.sum(
                            jnp.where(extra_lane == head_id * heads + h, all_cum, 0.0),
                            axis=1,
                            keepdims=True,
                        ),
                        (rows_per_head, head_dim),
                    )
                    for h in range(heads)
                ],
                axis=1,
            )
            queries = jnp.concatenate([block[0:rows_per_head]] * heads, axis=0)
            spreads[group] = jnp.where(own_head, queries, 0.0).astype(BF16)
        for group in span:
            for copy in copies[group]:
                copy.wait()
        pairs = [(group, member) for group in span for member in range(members)]
        scores = {
            (group, member): lax.dot_general(
                spreads[group],
                keys_ref[group, member],
                (((1,), (1,)), ((), ())),
                preferred_element_type=F32,
            )
            for group, member in pairs
        }
        near = {
            group: lax.dot_general(
                spreads[group],
                blocks[group][rows_per_head : 2 * rows_per_head].astype(BF16),
                (((1,), (1,)), ((), ())),
                preferred_element_type=F32,
            )
            for group in span
        }
        weighed = {}
        for group, member in pairs:
            first = (group * members + member) * heads
            factor = jnp.concatenate(
                [
                    jnp.broadcast_to(factors[first + h : first + h + 1], (rows_per_head, length))
                    for h in range(heads)
                ],
                axis=0,
            )
            score = scores[group, member] * factor
            score = jnp.where((row_s % rows_per_head) // steps == member, score, 0.0)
            high = score.astype(BF16)
            low = (score - high.astype(F32)).astype(BF16)
            weighed[group, member] = jnp.concatenate([high, low], axis=0)
        sums = {
            (group, member): jnp.dot(
                weighed[group, member], values_ref[group, member], preferred_element_type=F32
            )
            for group, member in pairs
        }
        results = []
        for group in span:
            cum = cums[group]
            values = blocks[group][2 * rows_per_head : 3 * rows_per_head] * jnp.exp(-cum)
            total = jnp.dot(
                jnp.where(causal, near[group], 0.0),
                values,
                precision=HIGHEST,
                preferred_element_type=F32,
            )
            for member in range(members):
                both = sums[group, member]
                total = total + both[:rows] + both[rows:]
            total = jnp.where(own_head, total, 0.0)
            readout = total[0:rows_per_head]
            for h in range(1, heads):
                readout = readout + total[h * rows_per_head : (h + 1) * rows_per_head]
            readout = readout * jnp.exp(cum) * (1.0 / head_dim)
            squares = jnp.sum(readout * readout, axis=1, keepdims=True)
            high = squares.astype(BF16).astype(F32)
            extra = jnp.where(
                extra_lane == 0, high, jnp.where(extra_lane == 1, squares - high, 0.0)
            )
            results.append(jnp.concatenate([readout * gain, extra], axis=1))
        at = slice(start * rows_per_head, (start + half) * rows_per_head)
        out_ref[at, :] = jnp.concatenate(results, axis=0).astype(BF16)


def readout_features(k_pre, v_pre, decay, dec, gain):
    groups, members, length, width = k_pre.shape
    count = groups * dec.shape[1] // 4
    return pl.pallas_call(
        readout_kernel,
        in_specs=in_hbm(4) + whole(1),
        out_specs=whole(1)[0],
        out_shape=jax.ShapeDtypeStruct((count, width + EXTRA), BF16),
        scratch_shapes=[
            pltpu.VMEM(k_pre.shape, BF16),
            pltpu.VMEM(v_pre.shape, BF16),
            pltpu.VMEM(decay.shape, F32),
            pltpu.VMEM(gain.shape, F32),
            pltpu.SemaphoreType.DMA((2 * groups + 2,)),
        ],
        compiler_params=pltpu.CompilerParams(vmem_limit_bytes=14 << 20),
        cost_estimate=pl.CostEstimate(
            flops=2 * 2 * 64 * groups * members * length * width,
            bytes_accessed=4 * groups * members * length * width,
            transcendentals=0,
        ),
    )(*pin(k_pre, v_pre, decay, gain), dec)


def stage_kernel(source_hbm, out_ref, sems):
    pieces = sems.shape[0]
    rows = out_ref.shape[0] // pieces
    copies = [
        pltpu.make_async_copy(
            source_hbm.at[pl.ds(i * rows, rows)], out_ref.at[pl.ds(i * rows, rows)], sems.at[i]
        )
        for i in range(pieces)
    ]
    for copy in copies:
        copy.start()
    for copy in copies:
        copy.wait()


def stage(weights):
    return pl.pallas_call(
        stage_kernel,
        in_specs=in_hbm(1),
        out_specs=whole(1)[0],
        out_shape=jax.ShapeDtypeStruct(weights.shape, weights.dtype),
        scratch_shapes=[pltpu.SemaphoreType.DMA((4,))],
        compiler_params=pltpu.CompilerParams(vmem_limit_bytes=2 << 20),
        cost_estimate=pl.CostEstimate(
            flops=0, bytes_accessed=2 * weights.size * 2, transcendentals=0
        ),
    )(*pin(weights))


def project_kernel(features_ref, own_ref, other_ref, out_ref):
    half, model_dim = own_ref.shape
    first = lax.axis_index("exp") % 2 == 0
    low, high = features_ref[:, 0:half], features_ref[:, half : 2 * half]
    mine = jnp.where(first, low, high)
    theirs = jnp.where(first, high, low)
    piece = model_dim // 2
    for at in (slice(0, piece), slice(piece, model_dim)):
        out_ref[:, at] = (
            jnp.dot(mine, own_ref[:, at], preferred_element_type=F32)
            + jnp.dot(theirs, other_ref[:, at], preferred_element_type=F32)
        ).astype(BF16)
    out_ref[:, model_dim:] = features_ref[:, 2 * half : 2 * half + EXTRA]


def project(features, own, other):
    count = features.shape[0]
    half, model_dim = own.shape
    return pl.pallas_call(
        project_kernel,
        in_specs=whole(3),
        out_specs=whole(1)[0],
        out_shape=pltpu.HBM((count, model_dim + EXTRA), BF16),
        compiler_params=pltpu.CompilerParams(vmem_limit_bytes=8 << 20),
        cost_estimate=pl.CostEstimate(
            flops=4 * count * half * model_dim,
            bytes_accessed=4 * half * model_dim,
            transcendentals=0,
        ),
    )(features, own, other)


def inward_kernel(rows_ref, w_in_ref, hidden_ref):
    depth = rows_ref.shape[1] // 2
    total = jnp.dot(rows_ref[:, :depth], w_in_ref[:depth, :], preferred_element_type=F32)
    hidden_ref[...] = total
    hidden_ref[...] += jnp.dot(rows_ref[:, depth:], w_in_ref[depth:, :], preferred_element_type=F32)


def inward(rows, w_in):
    count, model_dim = rows.shape
    hidden = w_in.shape[1]
    return pl.pallas_call(
        inward_kernel,
        in_specs=whole(2),
        out_specs=whole(1)[0],
        out_shape=pltpu.VMEM((count, hidden), F32),
        compiler_params=pltpu.CompilerParams(vmem_limit_bytes=6 << 20),
        cost_estimate=pl.CostEstimate(
            flops=2 * count * model_dim * hidden,
            bytes_accessed=2 * model_dim * hidden + 2 * count * model_dim,
            transcendentals=0,
        ),
    )(rows, w_in)


def middle_kernel(early_ref, rows_ref, order_ref, w_in_ref, w_out_ref, active_ref, last_ref):
    late = jnp.dot(rows_ref[...], w_in_ref[...], preferred_element_type=F32)
    hidden = jnp.concatenate([early_ref[...], late], axis=0)
    active = (hidden * jax.nn.sigmoid(hidden)).astype(BF16)
    active = jnp.dot(order_ref[...], active, preferred_element_type=F32).astype(BF16)
    active_ref[...] = active
    last = active[early_ref.shape[0] :]
    last_ref[...] = jnp.dot(last, w_out_ref[...], preferred_element_type=F32).astype(BF16)


def middle(early, rows, order, w_in, w_out):
    count, model_dim = rows.shape
    hidden = w_in.shape[1]
    total = early.shape[0] + count
    return pl.pallas_call(
        middle_kernel,
        in_specs=whole(5),
        out_specs=whole(2),
        out_shape=[
            pltpu.VMEM((total, hidden), BF16),
            pltpu.VMEM((count, model_dim), BF16),
        ],
        compiler_params=pltpu.CompilerParams(vmem_limit_bytes=6 << 20),
        cost_estimate=pl.CostEstimate(
            flops=4 * count * model_dim * hidden,
            bytes_accessed=4 * model_dim * hidden,
            transcendentals=total * hidden,
        ),
    )(early, rows, order, w_in, w_out)


def outward_kernel(active_ref, w_out_ref, out_ref):
    rows, model_dim = out_ref.shape
    piece = model_dim // 3
    active = active_ref[0:rows, :]
    for i in range(3):
        at = slice(i * piece, (i + 1) * piece)
        out_ref[:, at] = jnp.dot(
            active, w_out_ref[:, at], preferred_element_type=F32
        ).astype(BF16)


def outward(active, w_out, count):
    hidden, model_dim = w_out.shape
    return pl.pallas_call(
        outward_kernel,
        in_specs=whole(2),
        out_specs=whole(1)[0],
        out_shape=pltpu.VMEM((count, model_dim), BF16),
        compiler_params=pltpu.CompilerParams(vmem_limit_bytes=6 << 20),
        cost_estimate=pl.CostEstimate(
            flops=2 * count * model_dim * hidden,
            bytes_accessed=2 * model_dim * hidden + 2 * count * model_dim,
            transcendentals=0,
        ),
    )(active, w_out)


def gather_heads(own, w_in, w_out, aside):
    own, w_in, w_out = lax.optimization_barrier((own, w_in, w_out))
    from_down = send(own, Z_UP)
    from_up = send(own, Z_DOWN)
    far = send(own, Z_FAR)
    beside = send(own, Y_LO)
    w_in, w_out = stage(w_in), stage(w_out)
    aside = send(aside, SWAP)
    beside, far, aside = lax.optimization_barrier((beside, far, aside))
    beside_down = send(beside, Z_UP)
    beside_up = send(beside, Z_DOWN)
    beside_far = send(far, Y_LO)
    early = inward(jnp.concatenate([own, from_up, from_down, far, beside]), w_in)
    late = jnp.concatenate([beside_up, beside_down, beside_far])
    return early, late, w_in, w_out, aside


def add(first, *others):
    total = first.astype(F32)
    for other in others:
        total = total + other.astype(F32)
    return total.astype(BF16)


def last_sum_kernel(parts_ref, *refs):
    out_ref = refs[-1]
    total = parts_ref[0 : refs[0].shape[0], :].astype(F32)
    for ref in refs[:-1]:
        total = total + ref[...].astype(F32)
    for i in range(out_ref.shape[0]):
        out_ref[i] = total[CAP * i : CAP * (i + 1)].astype(BF16)


def scatter_heads(parts, last):
    rows, width = last.shape[0] // 3, last.shape[1]

    def block(i):
        return parts[i * rows : (i + 1) * rows]

    first = send(last[:rows], Z_UP)
    second = send(last[rows : 2 * rows], Z_DOWN)
    third = send(last[2 * rows :], Y_LO)
    from_down = send(block(1), Z_UP)
    from_up = send(block(2), Z_DOWN)
    from_far = send(add(block(3), third), Z_FAR)
    from_beside = send(add(block(4), first, second), Y_LO)
    return pl.pallas_call(
        last_sum_kernel,
        in_specs=whole(5),
        out_specs=whole(1)[0],
        out_shape=pltpu.HBM((rows // CAP, CAP, width), BF16),
        compiler_params=pltpu.CompilerParams(vmem_limit_bytes=6 << 20),
        cost_estimate=pl.CostEstimate(
            flops=0, bytes_accessed=12 * rows * width, transcendentals=0
        ),
    )(parts, from_down, from_up, from_far, from_beside)


def finish_kernel(returned_ref, resid_ref, weights_ref, out_ref):
    members, steps, width = out_ref.shape[1:]
    tokens = members * steps
    slots = weights_ref.shape[1]
    copies = returned_ref.shape[0] // slots
    piece = width // 4
    for i in range(4):
        at = slice(i * piece, (i + 1) * piece)
        total = returned_ref[0:slots, at].astype(F32)
        for copy in range(1, copies):
            total = total + returned_ref[copy * slots : (copy + 1) * slots, at].astype(F32)
        mixed = jnp.dot(weights_ref[...], total.astype(BF16), preferred_element_type=F32)
        mixed = mixed[:tokens] + mixed[tokens:]
        decoded = resid_ref[:, at].astype(F32) + mixed
        for member in range(members):
            out_ref[0, member, :, at] = decoded[member * steps : (member + 1) * steps].astype(BF16)


def finish(returned, resid, weights, members, steps, width):
    return pl.pallas_call(
        finish_kernel,
        in_specs=whole(3),
        out_specs=whole(1)[0],
        out_shape=jax.ShapeDtypeStruct((1, members, steps, width), BF16),
        compiler_params=pltpu.CompilerParams(vmem_limit_bytes=6 << 20),
    )(returned, resid, weights)


def on_device(
    k_pre,
    v_pre,
    pre_decay,
    q_dec,
    k_dec,
    v_dec,
    dec_decay,
    x_dec,
    route,
    att_gain,
    w_o,
    ffn_gain,
    w_router,
    w_in,
    w_out,
):
    head_id = lax.axis_index("head")
    n_head, n_exp = lax.axis_size("head"), lax.axis_size("exp")
    owned, steps, width = q_dec.shape[1:]
    tokens = owned * steps
    model_dim = x_dec.shape[3]

    w_o_other = send(w_o, CORE)

    packed = pack_decode(q_dec, k_dec, v_dec, dec_decay, n_head)
    packed = lax.all_to_all(packed, "head", split_axis=0, concat_axis=0, tiled=True)
    features = readout_features(
        k_pre, v_pre, jnp.transpose(pre_decay, (0, 1, 3, 2)), packed, att_gain[None]
    )

    ids = route.reshape(tokens, 2)
    carried = jnp.concatenate(
        [
            x_dec.reshape(tokens, model_dim),
            jnp.pad(ids.astype(BF16), ((0, 0), (0, EXTRA - 2))),
        ],
        axis=1,
    )
    features, carried, w_o_other = lax.optimization_barrier((features, carried, w_o_other))
    features = send(features, SWAP)
    carried = send(carried, SWAP)
    x_here = carried[:, :model_dim]
    ids_here = carried[:, model_dim : model_dim + 2].astype(jnp.int32)
    w_o_other = stage(w_o_other)
    partial_sum = project(features, w_o, w_o_other)
    partial_sum = partial_sum.reshape(n_head, tokens, model_dim + EXTRA)
    parts = lax.all_to_all(
        partial_sum,
        "exp",
        split_axis=0,
        concat_axis=0,
        tiled=True,
        axis_index_groups=[list(range(c, n_exp, 2)) for c in range(2)],
    )
    summed = jnp.sum(parts.astype(F32), axis=0)
    squares = summed[:, model_dim : model_dim + 1] + summed[:, model_dim + 1 : model_dim + 2]
    attn = summed[:, :model_dim] * lax.rsqrt(squares / width + 1e-06)
    resid = (x_here.astype(F32) + attn).astype(BF16)
    resid_f = resid.astype(F32)
    mean_square = jnp.mean(resid_f * resid_f, axis=-1, keepdims=True)
    ffn_in = (resid_f * lax.rsqrt(mean_square + 1e-06) * ffn_gain).astype(BF16)

    experts = w_router.shape[1]
    logits = jnp.dot(ffn_in, w_router, preferred_element_type=F32)

    def slots_of(expert_ids):
        flat_ids = expert_ids.reshape(-1)
        order = jnp.arange(flat_ids.shape[0], dtype=jnp.int32)
        earlier = (flat_ids[:, None] == flat_ids[None, :]) & (order[:, None] > order[None, :])
        slots = jnp.sum(earlier.astype(jnp.int32), axis=1)
        target = (flat_ids * CAP + slots).reshape(tokens, 2)
        places = jnp.arange(experts * CAP, dtype=jnp.int32)
        return places[None, None, :] == target[:, :, None]

    table = jnp.sum(slots_of(ids_here).astype(F32), axis=1).astype(BF16)
    rows = jnp.dot(table.T, ffn_in, preferred_element_type=F32).astype(BF16)
    rows = rows.reshape(n_exp, CAP, model_dim)
    onehot = (ids_here[:, :, None] == jnp.arange(experts, dtype=jnp.int32)).astype(F32)
    gates = jax.nn.sigmoid(jnp.sum(onehot * logits[:, None, :], axis=-1))
    weights = gates / jnp.sum(gates, axis=-1, keepdims=True)
    weight_parts = jnp.concatenate(split_two(weights), axis=1)

    rows = lax.all_to_all(rows, "exp", split_axis=0, concat_axis=0, tiled=True)
    back = jnp.concatenate([resid, jnp.pad(weight_parts, ((0, 0), (0, EXTRA - 4)))], axis=1)
    early, late, near_in, near_out, back = gather_heads(
        rows.reshape(n_exp * CAP, model_dim), w_in[0], w_out[0], back
    )

    count = n_head * n_exp * CAP
    per_group = count // n_head // n_head
    offsets = jnp.array([0, 2, 6, 4, 1, 3, 7, 5], jnp.int32)

    def position(relative):
        step = offsets[relative]
        return ((head_id // 2 + step // 2) % 4) * 2 + (head_id % 2 + step % 2) % 2

    leaving = jnp.arange(count, dtype=jnp.int32)
    block = n_head * per_group
    goes_to = position(leaving // block)
    came_from = (leaving % block) // per_group
    key_out = (came_from * n_head + goes_to) * per_group + leaving % per_group
    key_in = (position(leaving // block) * n_head + (leaving % block) // per_group) * per_group
    key_in = key_in + leaving % per_group
    order = (key_out[:, None] == key_in[None, :]).astype(BF16)
    active, last = middle(early, late, order, near_in, near_out)
    outputs = scatter_heads(outward(active, near_out, early.shape[0]), last)
    returned = lax.all_to_all(
        outputs, "exp", split_axis=0, concat_axis=0, tiled=True
    ).reshape(n_exp * CAP, model_dim)

    weights_here = back[:, model_dim : model_dim + 2].astype(F32)
    weights_here = weights_here + back[:, model_dim + 2 : model_dim + 4].astype(F32)
    spread = jnp.sum(slots_of(ids).astype(F32) * weights_here[:, :, None], axis=1)
    spread = jnp.concatenate(split_two(spread), axis=0)
    return finish(returned, back, spread, owned, steps, model_dim)


def solution(mesh):
    return jax.shard_map(
        on_device,
        mesh=mesh,
        in_specs=(
            P(None, "exp", None, "head"),
            P(None, "exp", None, "head"),
            P(None, "exp", None, "head"),
            P("head", "exp", None, None),
            P("head", "exp", None, None),
            P("head", "exp", None, None),
            P("head", "exp", None, None),
            P("head", "exp", None, None),
            P("head", "exp", None, None),
            P(),
            P("exp", None),
            P(),
            P(),
            P("exp", None, "head"),
            P("exp", "head", None),
        ),
        out_specs=P("head", "exp", None, None),
        check_vma=False,
    )
```

```python
import jax
import jax.numpy as jnp
from jax import lax
from jax.experimental import pallas as pl
from jax.experimental.pallas import tpu as pltpu
from jax.sharding import PartitionSpec as P

CAP = 2
EXTRA = 128
AXES = ("head", "exp")
F32 = jnp.float32
BF16 = jnp.bfloat16
HIGHEST = lax.Precision.HIGHEST


def device_pairs(move):
    pairs = []
    for head in range(8):
        for exp in range(16):
            to_head, to_exp = move(head, exp)
            pairs.append((head * 16 + exp, to_head * 16 + to_exp))
    return pairs


CORE = device_pairs(lambda head, exp: (head, exp ^ 1))
Y_LO = device_pairs(lambda head, exp: (head ^ 1, exp))
Z_UP = device_pairs(lambda head, exp: ((head + 2) % 8, exp))
Z_DOWN = device_pairs(lambda head, exp: ((head + 6) % 8, exp))
Z_FAR = device_pairs(lambda head, exp: ((head + 4) % 8, exp))
SWAP = device_pairs(lambda head, exp: (exp // 2, 2 * head + exp % 2))


def send(value, pairs):
    return lax.ppermute(value, AXES, pairs)


def split_two(value):
    high = lax.reduce_precision(value, 8, 7)
    return high.astype(BF16), (value - high).astype(BF16)


def whole(count):
    return [pl.BlockSpec(memory_space=pltpu.VMEM)] * count


def pack_kernel(
    queries_hbm,
    keys_hbm,
    values_hbm,
    decay_hbm,
    out_ref,
    queries_ref,
    keys_ref,
    values_ref,
    decay_ref,
    sems,
):
    sources = (queries_hbm, keys_hbm, values_hbm, decay_hbm)
    targets = (queries_ref, keys_ref, values_ref, decay_ref)
    copies = [
        pltpu.make_async_copy(source, target, sems.at[i])
        for i, (source, target) in enumerate(zip(sources, targets))
    ]
    for copy in copies:
        copy.start()
    for copy in copies:
        copy.wait()
    blocks, _, width = out_ref.shape
    members, steps = decay_ref.shape[1], decay_ref.shape[2]
    rows = []
    for member in range(members):
        running = decay_ref[0, member, 0:1]
        rows.append(running)
        for step in range(1, steps):
            running = running + decay_ref[0, member, step : step + 1]
            rows.append(running)
    summed = jnp.concatenate(rows, axis=0)
    count = members * steps
    heads = summed.shape[1]
    summed = jnp.concatenate([summed, jnp.zeros((count, 128 - heads), F32)], axis=1)
    high = summed.astype(BF16).astype(F32)
    rest = summed - high
    middle = rest.astype(BF16).astype(F32)
    pieces = [high, middle, rest - middle]
    if width > 384:
        pieces.append(jnp.zeros((count, width - 384), F32))
    decays = jnp.concatenate(pieces, axis=1)
    arrays = [
        jnp.concatenate([ref[0, m].astype(F32) for m in range(members)], axis=0)
        for ref in (queries_ref, keys_ref, values_ref)
    ]
    for block in range(blocks):
        lanes = slice(block * width, (block + 1) * width)
        out_ref[block] = jnp.concatenate(
            [array[:, lanes] for array in arrays] + [decays], axis=0
        ).astype(BF16)


def in_hbm(count):
    return [pl.BlockSpec(memory_space=pltpu.MemorySpace.HBM)] * count


def pin(*arrays):
    return [pltpu.with_memory_space_constraint(array, pltpu.MemorySpace.HBM) for array in arrays]


def pack_decode(q_dec, k_dec, v_dec, dec_decay, blocks):
    members, steps, width = q_dec.shape[1:]
    return pl.pallas_call(
        pack_kernel,
        in_specs=in_hbm(4),
        out_specs=whole(1)[0],
        out_shape=pltpu.HBM((blocks, 4 * members * steps, width // blocks), BF16),
        scratch_shapes=[pltpu.VMEM(array.shape, array.dtype) for array in (q_dec, k_dec, v_dec, dec_decay)]
        + [pltpu.SemaphoreType.DMA((4,))],
        compiler_params=pltpu.CompilerParams(vmem_limit_bytes=6 << 20),
    )(*pin(q_dec, k_dec, v_dec, dec_decay))


def readout_kernel(
    keys_hbm,
    values_hbm,
    decay_hbm,
    gain_hbm,
    dec_ref,
    out_ref,
    keys_ref,
    values_ref,
    decay_ref,
    gain_ref,
    sems,
):
    groups, members = keys_ref.shape[0], keys_ref.shape[1]
    heads = decay_ref.shape[2]
    length = decay_ref.shape[3]
    width = keys_ref.shape[3]
    head_dim = width // heads
    rows_per_head = dec_ref.shape[1] // 4
    steps = rows_per_head // members
    rows = heads * rows_per_head
    head_id = lax.axis_index("head")
    decay_copy = pltpu.make_async_copy(decay_hbm, decay_ref, sems.at[2 * groups])
    decay_copy.start()
    gain_copy = pltpu.make_async_copy(gain_hbm, gain_ref, sems.at[2 * groups + 1])
    gain_copy.start()
    copies = []
    for group in range(groups):
        copies.append(
            (
                pltpu.make_async_copy(keys_hbm.at[group], keys_ref.at[group], sems.at[group]),
                pltpu.make_async_copy(
                    values_hbm.at[group], values_ref.at[group], sems.at[groups + group]
                ),
            )
        )
        for copy in copies[-1]:
            copy.start()
    earlier = lax.broadcasted_iota(jnp.int32, (length, length), 0)
    later = lax.broadcasted_iota(jnp.int32, (length, length), 1)
    after = (earlier > later).astype(F32)
    row = lax.broadcasted_iota(jnp.int32, (rows, width), 0)
    lane = lax.broadcasted_iota(jnp.int32, (rows, width), 1)
    own_head = (row // rows_per_head) == (lane // head_dim)
    row_s = lax.broadcasted_iota(jnp.int32, (rows, length), 0)
    row_d = lax.broadcasted_iota(jnp.int32, (rows, rows_per_head), 0) % rows_per_head
    col_d = lax.broadcasted_iota(jnp.int32, (rows, rows_per_head), 1)
    causal = ((row_d // steps) == (col_d // steps)) & ((col_d % steps) <= (row_d % steps))
    extra_lane = lax.broadcasted_iota(jnp.int32, (rows_per_head, EXTRA), 1)
    decay_copy.wait()
    gain_copy.wait()
    gain = gain_ref[:, pl.ds(pl.multiple_of(head_id * width, width), width)]
    summed = jnp.concatenate(
        [decay_ref[g, m] for g in range(groups) for m in range(members)], axis=0
    )
    factors = jnp.exp(jnp.dot(summed, after, precision=HIGHEST, preferred_element_type=F32))

    half = groups // 2
    for start in (0, half):
        span = range(start, start + half)
        cums, spreads, blocks = {}, {}, {}
        for group in span:
            block = dec_ref[group].astype(F32)
            blocks[group] = block
            parts = block[3 * rows_per_head : 4 * rows_per_head]
            all_cum = parts[:, 0:128] + parts[:, 128:256] + parts[:, 256:384]
            cums[group] = jnp.concatenate(
                [
                    jnp.broadcast_to(
                        jnp.sum(
                            jnp.where(extra_lane == head_id * heads + h, all_cum, 0.0),
                            axis=1,
                            keepdims=True,
                        ),
                        (rows_per_head, head_dim),
                    )
                    for h in range(heads)
                ],
                axis=1,
            )
            queries = jnp.concatenate([block[0:rows_per_head]] * heads, axis=0)
            spreads[group] = jnp.where(own_head, queries, 0.0).astype(BF16)
        for group in span:
            for copy in copies[group]:
                copy.wait()
        pairs = [(group, member) for group in span for member in range(members)]
        scores = {
            (group, member): lax.dot_general(
                spreads[group],
                keys_ref[group, member],
                (((1,), (1,)), ((), ())),
                preferred_element_type=F32,
            )
            for group, member in pairs
        }
        near = {
            group: lax.dot_general(
                spreads[group],
                blocks[group][rows_per_head : 2 * rows_per_head].astype(BF16),
                (((1,), (1,)), ((), ())),
                preferred_element_type=F32,
            )
            for group in span
        }
        weighed = {}
        for group, member in pairs:
            first = (group * members + member) * heads
            factor = jnp.concatenate(
                [
                    jnp.broadcast_to(factors[first + h : first + h + 1], (rows_per_head, length))
                    for h in range(heads)
                ],
                axis=0,
            )
            score = scores[group, member] * factor
            score = jnp.where((row_s % rows_per_head) // steps == member, score, 0.0)
            high = score.astype(BF16)
            low = (score - high.astype(F32)).astype(BF16)
            weighed[group, member] = jnp.concatenate([high, low], axis=0)
        sums = {
            (group, member): jnp.dot(
                weighed[group, member], values_ref[group, member], preferred_element_type=F32
            )
            for group, member in pairs
        }
        results = []
        for group in span:
            cum = cums[group]
            values = blocks[group][2 * rows_per_head : 3 * rows_per_head] * jnp.exp(-cum)
            total = jnp.dot(
                jnp.where(causal, near[group], 0.0),
                values,
                precision=HIGHEST,
                preferred_element_type=F32,
            )
            for member in range(members):
                both = sums[group, member]
                total = total + both[:rows] + both[rows:]
            total = jnp.where(own_head, total, 0.0)
            readout = total[0:rows_per_head]
            for h in range(1, heads):
                readout = readout + total[h * rows_per_head : (h + 1) * rows_per_head]
            readout = readout * jnp.exp(cum) * (1.0 / head_dim)
            squares = jnp.sum(readout * readout, axis=1, keepdims=True)
            high = squares.astype(BF16).astype(F32)
            extra = jnp.where(
                extra_lane == 0, high, jnp.where(extra_lane == 1, squares - high, 0.0)
            )
            results.append(jnp.concatenate([readout * gain, extra], axis=1))
        at = slice(start * rows_per_head, (start + half) * rows_per_head)
        out_ref[at, :] = jnp.concatenate(results, axis=0).astype(BF16)


def readout_features(k_pre, v_pre, decay, dec, gain):
    groups, members, length, width = k_pre.shape
    count = groups * dec.shape[1] // 4
    return pl.pallas_call(
        readout_kernel,
        in_specs=in_hbm(4) + whole(1),
        out_specs=whole(1)[0],
        out_shape=jax.ShapeDtypeStruct((count, width + EXTRA), BF16),
        scratch_shapes=[
            pltpu.VMEM(k_pre.shape, BF16),
            pltpu.VMEM(v_pre.shape, BF16),
            pltpu.VMEM(decay.shape, F32),
            pltpu.VMEM(gain.shape, F32),
            pltpu.SemaphoreType.DMA((2 * groups + 2,)),
        ],
        compiler_params=pltpu.CompilerParams(vmem_limit_bytes=14 << 20),
        cost_estimate=pl.CostEstimate(
            flops=2 * 2 * 64 * groups * members * length * width,
            bytes_accessed=4 * groups * members * length * width,
            transcendentals=0,
        ),
    )(*pin(k_pre, v_pre, decay, gain), dec)


def stage_kernel(source_hbm, out_ref, sems):
    pieces = sems.shape[0]
    rows = out_ref.shape[0] // pieces
    copies = [
        pltpu.make_async_copy(
            source_hbm.at[pl.ds(i * rows, rows)], out_ref.at[pl.ds(i * rows, rows)], sems.at[i]
        )
        for i in range(pieces)
    ]
    for copy in copies:
        copy.start()
    for copy in copies:
        copy.wait()


def stage(weights):
    return pl.pallas_call(
        stage_kernel,
        in_specs=in_hbm(1),
        out_specs=whole(1)[0],
        out_shape=jax.ShapeDtypeStruct(weights.shape, weights.dtype),
        scratch_shapes=[pltpu.SemaphoreType.DMA((4,))],
        compiler_params=pltpu.CompilerParams(vmem_limit_bytes=2 << 20),
        cost_estimate=pl.CostEstimate(
            flops=0, bytes_accessed=2 * weights.size * 2, transcendentals=0
        ),
    )(*pin(weights))


def project_kernel(features_ref, own_ref, other_ref, out_ref):
    half, model_dim = own_ref.shape
    first = lax.axis_index("exp") % 2 == 0
    low, high = features_ref[:, 0:half], features_ref[:, half : 2 * half]
    mine = jnp.where(first, low, high)
    theirs = jnp.where(first, high, low)
    piece = model_dim // 2
    for at in (slice(0, piece), slice(piece, model_dim)):
        out_ref[:, at] = (
            jnp.dot(mine, own_ref[:, at], preferred_element_type=F32)
            + jnp.dot(theirs, other_ref[:, at], preferred_element_type=F32)
        ).astype(BF16)
    out_ref[:, model_dim:] = features_ref[:, 2 * half : 2 * half + EXTRA]


def project(features, own, other):
    count = features.shape[0]
    half, model_dim = own.shape
    return pl.pallas_call(
        project_kernel,
        in_specs=whole(3),
        out_specs=whole(1)[0],
        out_shape=pltpu.HBM((count, model_dim + EXTRA), BF16),
        compiler_params=pltpu.CompilerParams(vmem_limit_bytes=8 << 20),
        cost_estimate=pl.CostEstimate(
            flops=4 * count * half * model_dim,
            bytes_accessed=4 * half * model_dim,
            transcendentals=0,
        ),
    )(features, own, other)


def inward_kernel(rows_ref, w_in_ref, hidden_ref):
    depth = rows_ref.shape[1] // 2
    total = jnp.dot(rows_ref[:, :depth], w_in_ref[:depth, :], preferred_element_type=F32)
    hidden_ref[...] = total
    hidden_ref[...] += jnp.dot(rows_ref[:, depth:], w_in_ref[depth:, :], preferred_element_type=F32)


def inward(rows, w_in):
    count, model_dim = rows.shape
    hidden = w_in.shape[1]
    return pl.pallas_call(
        inward_kernel,
        in_specs=whole(2),
        out_specs=whole(1)[0],
        out_shape=pltpu.VMEM((count, hidden), F32),
        compiler_params=pltpu.CompilerParams(vmem_limit_bytes=6 << 20),
        cost_estimate=pl.CostEstimate(
            flops=2 * count * model_dim * hidden,
            bytes_accessed=2 * model_dim * hidden + 2 * count * model_dim,
            transcendentals=0,
        ),
    )(rows, w_in)


def middle_kernel(early_ref, rows_ref, order_ref, w_in_ref, w_out_ref, active_ref, *last_refs):
    late = jnp.dot(rows_ref[...], w_in_ref[...], preferred_element_type=F32)
    hidden = jnp.concatenate([early_ref[...], late], axis=0)
    active = (hidden * jax.nn.sigmoid(hidden)).astype(BF16)
    active = jnp.dot(order_ref[...], active, preferred_element_type=F32).astype(BF16)
    active_ref[...] = active
    write_blocks(active[early_ref.shape[0] :], w_out_ref, last_refs, 2)


def write_blocks(active, w_out_ref, refs, pieces):
    rows, model_dim = refs[0].shape
    piece = model_dim // pieces
    for i in range(pieces):
        at = slice(i * piece, (i + 1) * piece)
        result = jnp.dot(active, w_out_ref[:, at], preferred_element_type=F32)
        for j, ref in enumerate(refs):
            ref[:, at] = result[j * rows : (j + 1) * rows].astype(BF16)


def middle(early, rows, order, w_in, w_out, block):
    count, model_dim = rows.shape
    hidden = w_in.shape[1]
    total = early.shape[0] + count
    return pl.pallas_call(
        middle_kernel,
        in_specs=whole(5),
        out_specs=whole(1 + count // block),
        out_shape=[pltpu.VMEM((total, hidden), BF16)]
        + [pltpu.VMEM((block, model_dim), BF16)] * (count // block),
        compiler_params=pltpu.CompilerParams(vmem_limit_bytes=8 << 20),
        cost_estimate=pl.CostEstimate(
            flops=4 * count * model_dim * hidden,
            bytes_accessed=4 * model_dim * hidden,
            transcendentals=total * hidden,
        ),
    )(early, rows, order, w_in, w_out)


def outward_kernel(active_ref, w_out_ref, *out_refs):
    rows = len(out_refs) * out_refs[0].shape[0]
    write_blocks(active_ref[0:rows, :], w_out_ref, out_refs, 3)


def outward(active, w_out, blocks, block):
    hidden, model_dim = w_out.shape
    count = blocks * block
    return pl.pallas_call(
        outward_kernel,
        in_specs=whole(2),
        out_specs=whole(blocks),
        out_shape=[pltpu.VMEM((block, model_dim), BF16)] * blocks,
        compiler_params=pltpu.CompilerParams(vmem_limit_bytes=8 << 20),
        cost_estimate=pl.CostEstimate(
            flops=2 * count * model_dim * hidden,
            bytes_accessed=2 * model_dim * hidden + 2 * count * model_dim,
            transcendentals=0,
        ),
    )(active, w_out)


def gather_heads(own, w_in, w_out, aside):
    own, w_in, w_out = lax.optimization_barrier((own, w_in, w_out))
    from_down = send(own, Z_UP)
    from_up = send(own, Z_DOWN)
    far = send(own, Z_FAR)
    beside = send(own, Y_LO)
    w_in, w_out = stage(w_in), stage(w_out)
    aside = send(aside, SWAP)
    beside, far, aside = lax.optimization_barrier((beside, far, aside))
    beside_down = send(beside, Z_UP)
    beside_up = send(beside, Z_DOWN)
    beside_far = send(far, Y_LO)
    early = inward(jnp.concatenate([own, from_up, from_down, far, beside]), w_in)
    late = jnp.concatenate([beside_up, beside_down, beside_far])
    return early, late, w_in, w_out, aside


def sum_kernel(*refs):
    total = refs[0][...].astype(F32)
    for ref in refs[1:-1]:
        total = total + ref[...].astype(F32)
    refs[-1][...] = total.astype(BF16)


def add(*arrays):
    return pl.pallas_call(
        sum_kernel,
        in_specs=whole(len(arrays)),
        out_specs=whole(1)[0],
        out_shape=pltpu.VMEM(arrays[0].shape, BF16),
        compiler_params=pltpu.CompilerParams(vmem_limit_bytes=4 << 20),
    )(*arrays)


def last_sum_kernel(*refs):
    out_ref = refs[-1]
    total = refs[0][...].astype(F32)
    for ref in refs[1:-1]:
        total = total + ref[...].astype(F32)
    for i in range(out_ref.shape[0]):
        out_ref[i] = total[CAP * i : CAP * (i + 1)].astype(BF16)


def scatter_heads(own, up, down, far, beside, beside_up, beside_down, beside_far):
    rows, width = own.shape
    first = send(beside_up, Z_UP)
    second = send(beside_down, Z_DOWN)
    third = send(beside_far, Y_LO)
    from_far = send(add(far, third), Z_FAR)
    from_down = send(up, Z_UP)
    from_up = send(down, Z_DOWN)
    from_beside = send(add(beside, first, second), Y_LO)
    return pl.pallas_call(
        last_sum_kernel,
        in_specs=whole(5),
        out_specs=whole(1)[0],
        out_shape=pltpu.HBM((rows // CAP, CAP, width), BF16),
        compiler_params=pltpu.CompilerParams(vmem_limit_bytes=6 << 20),
        cost_estimate=pl.CostEstimate(
            flops=0, bytes_accessed=12 * rows * width, transcendentals=0
        ),
    )(own, from_down, from_up, from_far, from_beside)


def finish_kernel(returned_ref, resid_ref, weights_ref, out_ref):
    members, steps, width = out_ref.shape[1:]
    tokens = members * steps
    slots = weights_ref.shape[1]
    copies = returned_ref.shape[0] // slots
    piece = width // 4
    for i in range(4):
        at = slice(i * piece, (i + 1) * piece)
        total = returned_ref[0:slots, at].astype(F32)
        for copy in range(1, copies):
            total = total + returned_ref[copy * slots : (copy + 1) * slots, at].astype(F32)
        mixed = jnp.dot(weights_ref[...], total.astype(BF16), preferred_element_type=F32)
        mixed = mixed[:tokens] + mixed[tokens:]
        decoded = resid_ref[:, at].astype(F32) + mixed
        for member in range(members):
            out_ref[0, member, :, at] = decoded[member * steps : (member + 1) * steps].astype(BF16)


def finish(returned, resid, weights, members, steps, width):
    return pl.pallas_call(
        finish_kernel,
        in_specs=whole(3),
        out_specs=whole(1)[0],
        out_shape=jax.ShapeDtypeStruct((1, members, steps, width), BF16),
        compiler_params=pltpu.CompilerParams(vmem_limit_bytes=6 << 20),
    )(returned, resid, weights)


def on_device(
    k_pre,
    v_pre,
    pre_decay,
    q_dec,
    k_dec,
    v_dec,
    dec_decay,
    x_dec,
    route,
    att_gain,
    w_o,
    ffn_gain,
    w_router,
    w_in,
    w_out,
):
    head_id = lax.axis_index("head")
    n_head, n_exp = lax.axis_size("head"), lax.axis_size("exp")
    owned, steps, width = q_dec.shape[1:]
    tokens = owned * steps
    model_dim = x_dec.shape[3]

    w_o_other = send(w_o, CORE)

    packed = pack_decode(q_dec, k_dec, v_dec, dec_decay, n_head)
    packed = lax.all_to_all(packed, "head", split_axis=0, concat_axis=0, tiled=True)
    features = readout_features(
        k_pre, v_pre, jnp.transpose(pre_decay, (0, 1, 3, 2)), packed, att_gain[None]
    )

    ids = route.reshape(tokens, 2)
    carried = jnp.concatenate(
        [
            x_dec.reshape(tokens, model_dim),
            jnp.pad(ids.astype(BF16), ((0, 0), (0, EXTRA - 2))),
        ],
        axis=1,
    )
    features, carried, w_o_other = lax.optimization_barrier((features, carried, w_o_other))
    features = send(features, SWAP)
    carried = send(carried, SWAP)
    x_here = carried[:, :model_dim]
    ids_here = carried[:, model_dim : model_dim + 2].astype(jnp.int32)
    w_o_other = stage(w_o_other)
    partial_sum = project(features, w_o, w_o_other)
    partial_sum = partial_sum.reshape(n_head, tokens, model_dim + EXTRA)
    parts = lax.all_to_all(
        partial_sum,
        "exp",
        split_axis=0,
        concat_axis=0,
        tiled=True,
        axis_index_groups=[list(range(c, n_exp, 2)) for c in range(2)],
    )
    summed = jnp.sum(parts.astype(F32), axis=0)
    squares = summed[:, model_dim : model_dim + 1] + summed[:, model_dim + 1 : model_dim + 2]
    attn = summed[:, :model_dim] * lax.rsqrt(squares / width + 1e-06)
    resid = (x_here.astype(F32) + attn).astype(BF16)
    resid_f = resid.astype(F32)
    mean_square = jnp.mean(resid_f * resid_f, axis=-1, keepdims=True)
    ffn_in = (resid_f * lax.rsqrt(mean_square + 1e-06) * ffn_gain).astype(BF16)

    experts = w_router.shape[1]
    logits = jnp.dot(ffn_in, w_router, preferred_element_type=F32)

    def slots_of(expert_ids):
        flat_ids = expert_ids.reshape(-1)
        order = jnp.arange(flat_ids.shape[0], dtype=jnp.int32)
        earlier = (flat_ids[:, None] == flat_ids[None, :]) & (order[:, None] > order[None, :])
        slots = jnp.sum(earlier.astype(jnp.int32), axis=1)
        target = (flat_ids * CAP + slots).reshape(tokens, 2)
        places = jnp.arange(experts * CAP, dtype=jnp.int32)
        return places[None, None, :] == target[:, :, None]

    table = jnp.sum(slots_of(ids_here).astype(F32), axis=1).astype(BF16)
    rows = jnp.dot(table.T, ffn_in, preferred_element_type=F32).astype(BF16)
    rows = rows.reshape(n_exp, CAP, model_dim)
    onehot = (ids_here[:, :, None] == jnp.arange(experts, dtype=jnp.int32)).astype(F32)
    gates = jax.nn.sigmoid(jnp.sum(onehot * logits[:, None, :], axis=-1))
    weights = gates / jnp.sum(gates, axis=-1, keepdims=True)
    weight_parts = jnp.concatenate(split_two(weights), axis=1)

    rows = lax.all_to_all(rows, "exp", split_axis=0, concat_axis=0, tiled=True)
    back = jnp.concatenate([resid, jnp.pad(weight_parts, ((0, 0), (0, EXTRA - 4)))], axis=1)
    early, late, near_in, near_out, back = gather_heads(
        rows.reshape(n_exp * CAP, model_dim), w_in[0], w_out[0], back
    )

    count = n_head * n_exp * CAP
    per_group = count // n_head // n_head
    offsets = jnp.array([0, 2, 6, 4, 1, 3, 7, 5], jnp.int32)

    def position(relative):
        step = offsets[relative]
        return ((head_id // 2 + step // 2) % 4) * 2 + (head_id % 2 + step % 2) % 2

    leaving = jnp.arange(count, dtype=jnp.int32)
    block = n_head * per_group
    goes_to = position(leaving // block)
    came_from = (leaving % block) // per_group
    key_out = (came_from * n_head + goes_to) * per_group + leaving % per_group
    key_in = (position(leaving // block) * n_head + (leaving % block) // per_group) * per_group
    key_in = key_in + leaving % per_group
    order = (key_out[:, None] == key_in[None, :]).astype(BF16)
    active, *last = middle(early, late, order, near_in, near_out, block)
    outputs = scatter_heads(*outward(active, near_out, early.shape[0] // block, block), *last)
    returned = lax.all_to_all(
        outputs, "exp", split_axis=0, concat_axis=0, tiled=True
    ).reshape(n_exp * CAP, model_dim)

    weights_here = back[:, model_dim : model_dim + 2].astype(F32)
    weights_here = weights_here + back[:, model_dim + 2 : model_dim + 4].astype(F32)
    spread = jnp.sum(slots_of(ids).astype(F32) * weights_here[:, :, None], axis=1)
    spread = jnp.concatenate(split_two(spread), axis=0)
    return finish(returned, back, spread, owned, steps, model_dim)


def solution(mesh):
    return jax.shard_map(
        on_device,
        mesh=mesh,
        in_specs=(
            P(None, "exp", None, "head"),
            P(None, "exp", None, "head"),
            P(None, "exp", None, "head"),
            P("head", "exp", None, None),
            P("head", "exp", None, None),
            P("head", "exp", None, None),
            P("head", "exp", None, None),
            P("head", "exp", None, None),
            P("head", "exp", None, None),
            P(),
            P("exp", None),
            P(),
            P(),
            P("exp", None, "head"),
            P("exp", "head", None),
        ),
        out_specs=P("head", "exp", None, None),
        check_vma=False,
    )
```

```python
import jax
import jax.numpy as jnp
from jax import lax
from jax.experimental import pallas as pl
from jax.experimental.pallas import tpu as pltpu
from jax.sharding import PartitionSpec as P

CAP = 2
EXTRA = 128
AXES = ("head", "exp")
F32 = jnp.float32
BF16 = jnp.bfloat16
HIGHEST = lax.Precision.HIGHEST


def device_pairs(move):
    pairs = []
    for head in range(8):
        for exp in range(16):
            to_head, to_exp = move(head, exp)
            pairs.append((head * 16 + exp, to_head * 16 + to_exp))
    return pairs


CORE = device_pairs(lambda head, exp: (head, exp ^ 1))
Y_LO = device_pairs(lambda head, exp: (head ^ 1, exp))
Z_UP = device_pairs(lambda head, exp: ((head + 2) % 8, exp))
Z_DOWN = device_pairs(lambda head, exp: ((head + 6) % 8, exp))
Z_FAR = device_pairs(lambda head, exp: ((head + 4) % 8, exp))
SWAP = device_pairs(lambda head, exp: (exp // 2, 2 * head + exp % 2))


def send(value, pairs):
    return lax.ppermute(value, AXES, pairs)


def split_two(value):
    high = lax.reduce_precision(value, 8, 7)
    return high.astype(BF16), (value - high).astype(BF16)


def whole(count):
    return [pl.BlockSpec(memory_space=pltpu.VMEM)] * count


def pack_kernel(
    queries_hbm,
    keys_hbm,
    values_hbm,
    decay_hbm,
    out_ref,
    queries_ref,
    keys_ref,
    values_ref,
    decay_ref,
    sems,
):
    sources = (queries_hbm, keys_hbm, values_hbm, decay_hbm)
    targets = (queries_ref, keys_ref, values_ref, decay_ref)
    copies = [
        pltpu.make_async_copy(source, target, sems.at[i])
        for i, (source, target) in enumerate(zip(sources, targets))
    ]
    for copy in copies:
        copy.start()
    for copy in copies:
        copy.wait()
    blocks, _, width = out_ref.shape
    members, steps = decay_ref.shape[1], decay_ref.shape[2]
    rows = []
    for member in range(members):
        running = decay_ref[0, member, 0:1]
        rows.append(running)
        for step in range(1, steps):
            running = running + decay_ref[0, member, step : step + 1]
            rows.append(running)
    summed = jnp.concatenate(rows, axis=0)
    count = members * steps
    heads = summed.shape[1]
    summed = jnp.concatenate([summed, jnp.zeros((count, 128 - heads), F32)], axis=1)
    high = summed.astype(BF16).astype(F32)
    rest = summed - high
    middle = rest.astype(BF16).astype(F32)
    pieces = [high, middle, rest - middle]
    if width > 384:
        pieces.append(jnp.zeros((count, width - 384), F32))
    decays = jnp.concatenate(pieces, axis=1)
    arrays = [
        jnp.concatenate([ref[0, m].astype(F32) for m in range(members)], axis=0)
        for ref in (queries_ref, keys_ref, values_ref)
    ]
    for block in range(blocks):
        lanes = slice(block * width, (block + 1) * width)
        out_ref[block] = jnp.concatenate(
            [array[:, lanes] for array in arrays] + [decays], axis=0
        ).astype(BF16)


def in_hbm(count):
    return [pl.BlockSpec(memory_space=pltpu.MemorySpace.HBM)] * count


def pin(*arrays):
    return [pltpu.with_memory_space_constraint(array, pltpu.MemorySpace.HBM) for array in arrays]


def pack_decode(q_dec, k_dec, v_dec, dec_decay, blocks):
    members, steps, width = q_dec.shape[1:]
    return pl.pallas_call(
        pack_kernel,
        in_specs=in_hbm(4),
        out_specs=whole(1)[0],
        out_shape=pltpu.HBM((blocks, 4 * members * steps, width // blocks), BF16),
        scratch_shapes=[pltpu.VMEM(array.shape, array.dtype) for array in (q_dec, k_dec, v_dec, dec_decay)]
        + [pltpu.SemaphoreType.DMA((4,))],
        compiler_params=pltpu.CompilerParams(vmem_limit_bytes=6 << 20),
    )(*pin(q_dec, k_dec, v_dec, dec_decay))


def readout_kernel(
    keys_hbm,
    values_hbm,
    decay_hbm,
    gain_hbm,
    dec_ref,
    out_ref,
    keys_ref,
    values_ref,
    decay_ref,
    gain_ref,
    sems,
):
    groups, members = keys_ref.shape[0], keys_ref.shape[1]
    heads = decay_ref.shape[2]
    length = decay_ref.shape[3]
    width = keys_ref.shape[3]
    head_dim = width // heads
    rows_per_head = dec_ref.shape[1] // 4
    steps = rows_per_head // members
    rows = heads * rows_per_head
    head_id = lax.axis_index("head")
    decay_copy = pltpu.make_async_copy(decay_hbm, decay_ref, sems.at[2 * groups])
    decay_copy.start()
    gain_copy = pltpu.make_async_copy(gain_hbm, gain_ref, sems.at[2 * groups + 1])
    gain_copy.start()
    copies = []
    for group in range(groups):
        copies.append(
            (
                pltpu.make_async_copy(keys_hbm.at[group], keys_ref.at[group], sems.at[group]),
                pltpu.make_async_copy(
                    values_hbm.at[group], values_ref.at[group], sems.at[groups + group]
                ),
            )
        )
        for copy in copies[-1]:
            copy.start()
    earlier = lax.broadcasted_iota(jnp.int32, (length, length), 0)
    later = lax.broadcasted_iota(jnp.int32, (length, length), 1)
    after = (earlier > later).astype(F32)
    row = lax.broadcasted_iota(jnp.int32, (rows, width), 0)
    lane = lax.broadcasted_iota(jnp.int32, (rows, width), 1)
    own_head = (row // rows_per_head) == (lane // head_dim)
    row_s = lax.broadcasted_iota(jnp.int32, (rows, length), 0)
    row_d = lax.broadcasted_iota(jnp.int32, (rows, rows_per_head), 0) % rows_per_head
    col_d = lax.broadcasted_iota(jnp.int32, (rows, rows_per_head), 1)
    causal = ((row_d // steps) == (col_d // steps)) & ((col_d % steps) <= (row_d % steps))
    extra_lane = lax.broadcasted_iota(jnp.int32, (rows_per_head, EXTRA), 1)
    decay_copy.wait()
    gain_copy.wait()
    gain = gain_ref[:, pl.ds(pl.multiple_of(head_id * width, width), width)]
    summed = jnp.concatenate(
        [decay_ref[g, m] for g in range(groups) for m in range(members)], axis=0
    )
    factors = jnp.exp(jnp.dot(summed, after, precision=HIGHEST, preferred_element_type=F32))

    half = groups // 2
    for start in (0, half):
        span = range(start, start + half)
        cums, spreads, blocks = {}, {}, {}
        for group in span:
            block = dec_ref[group].astype(F32)
            blocks[group] = block
            parts = block[3 * rows_per_head : 4 * rows_per_head]
            all_cum = parts[:, 0:128] + parts[:, 128:256] + parts[:, 256:384]
            cums[group] = jnp.concatenate(
                [
                    jnp.broadcast_to(
                        jnp.sum(
                            jnp.where(extra_lane == head_id * heads + h, all_cum, 0.0),
                            axis=1,
                            keepdims=True,
                        ),
                        (rows_per_head, head_dim),
                    )
                    for h in range(heads)
                ],
                axis=1,
            )
            queries = jnp.concatenate([block[0:rows_per_head]] * heads, axis=0)
            spreads[group] = jnp.where(own_head, queries, 0.0).astype(BF16)
        for group in span:
            for copy in copies[group]:
                copy.wait()
        pairs = [(group, member) for group in span for member in range(members)]
        scores = {
            (group, member): lax.dot_general(
                spreads[group],
                keys_ref[group, member],
                (((1,), (1,)), ((), ())),
                preferred_element_type=F32,
            )
            for group, member in pairs
        }
        near = {
            group: lax.dot_general(
                spreads[group],
                blocks[group][rows_per_head : 2 * rows_per_head].astype(BF16),
                (((1,), (1,)), ((), ())),
                preferred_element_type=F32,
            )
            for group in span
        }
        weighed = {}
        for group, member in pairs:
            first = (group * members + member) * heads
            factor = jnp.concatenate(
                [
                    jnp.broadcast_to(factors[first + h : first + h + 1], (rows_per_head, length))
                    for h in range(heads)
                ],
                axis=0,
            )
            score = scores[group, member] * factor
            score = jnp.where((row_s % rows_per_head) // steps == member, score, 0.0)
            high = score.astype(BF16)
            low = (score - high.astype(F32)).astype(BF16)
            weighed[group, member] = jnp.concatenate([high, low], axis=0)
        sums = {
            (group, member): jnp.dot(
                weighed[group, member], values_ref[group, member], preferred_element_type=F32
            )
            for group, member in pairs
        }
        results = []
        for group in span:
            cum = cums[group]
            values = blocks[group][2 * rows_per_head : 3 * rows_per_head] * jnp.exp(-cum)
            total = jnp.dot(
                jnp.where(causal, near[group], 0.0),
                values,
                precision=HIGHEST,
                preferred_element_type=F32,
            )
            for member in range(members):
                both = sums[group, member]
                total = total + both[:rows] + both[rows:]
            total = jnp.where(own_head, total, 0.0)
            readout = total[0:rows_per_head]
            for h in range(1, heads):
                readout = readout + total[h * rows_per_head : (h + 1) * rows_per_head]
            readout = readout * jnp.exp(cum) * (1.0 / head_dim)
            squares = jnp.sum(readout * readout, axis=1, keepdims=True)
            high = squares.astype(BF16).astype(F32)
            extra = jnp.where(
                extra_lane == 0, high, jnp.where(extra_lane == 1, squares - high, 0.0)
            )
            results.append(jnp.concatenate([readout * gain, extra], axis=1))
        at = slice(start * rows_per_head, (start + half) * rows_per_head)
        out_ref[at, :] = jnp.concatenate(results, axis=0).astype(BF16)


def readout_features(k_pre, v_pre, decay, dec, gain):
    groups, members, length, width = k_pre.shape
    count = groups * dec.shape[1] // 4
    return pl.pallas_call(
        readout_kernel,
        in_specs=in_hbm(4) + whole(1),
        out_specs=whole(1)[0],
        out_shape=jax.ShapeDtypeStruct((count, width + EXTRA), BF16),
        scratch_shapes=[
            pltpu.VMEM(k_pre.shape, BF16),
            pltpu.VMEM(v_pre.shape, BF16),
            pltpu.VMEM(decay.shape, F32),
            pltpu.VMEM(gain.shape, F32),
            pltpu.SemaphoreType.DMA((2 * groups + 2,)),
        ],
        compiler_params=pltpu.CompilerParams(vmem_limit_bytes=14 << 20),
        cost_estimate=pl.CostEstimate(
            flops=2 * 2 * 64 * groups * members * length * width,
            bytes_accessed=4 * groups * members * length * width,
            transcendentals=0,
        ),
    )(*pin(k_pre, v_pre, decay, gain), dec)


def stage_kernel(source_hbm, out_ref, sems):
    pieces = sems.shape[0]
    rows = out_ref.shape[0] // pieces
    copies = [
        pltpu.make_async_copy(
            source_hbm.at[pl.ds(i * rows, rows)], out_ref.at[pl.ds(i * rows, rows)], sems.at[i]
        )
        for i in range(pieces)
    ]
    for copy in copies:
        copy.start()
    for copy in copies:
        copy.wait()


def stage(weights):
    return pl.pallas_call(
        stage_kernel,
        in_specs=in_hbm(1),
        out_specs=whole(1)[0],
        out_shape=jax.ShapeDtypeStruct(weights.shape, weights.dtype),
        scratch_shapes=[pltpu.SemaphoreType.DMA((4,))],
        compiler_params=pltpu.CompilerParams(vmem_limit_bytes=2 << 20),
        cost_estimate=pl.CostEstimate(
            flops=0, bytes_accessed=2 * weights.size * 2, transcendentals=0
        ),
    )(*pin(weights))


def project_kernel(features_ref, own_ref, other_ref, out_ref):
    half, model_dim = own_ref.shape
    first = lax.axis_index("exp") % 2 == 0
    low, high = features_ref[:, 0:half], features_ref[:, half : 2 * half]
    mine = jnp.where(first, low, high)
    theirs = jnp.where(first, high, low)
    piece = model_dim // 2
    for at in (slice(0, piece), slice(piece, model_dim)):
        out_ref[:, at] = (
            jnp.dot(mine, own_ref[:, at], preferred_element_type=F32)
            + jnp.dot(theirs, other_ref[:, at], preferred_element_type=F32)
        ).astype(BF16)
    out_ref[:, model_dim:] = features_ref[:, 2 * half : 2 * half + EXTRA]


def project(features, own, other):
    count = features.shape[0]
    half, model_dim = own.shape
    return pl.pallas_call(
        project_kernel,
        in_specs=whole(3),
        out_specs=whole(1)[0],
        out_shape=pltpu.HBM((count, model_dim + EXTRA), BF16),
        compiler_params=pltpu.CompilerParams(vmem_limit_bytes=8 << 20),
        cost_estimate=pl.CostEstimate(
            flops=4 * count * half * model_dim,
            bytes_accessed=4 * half * model_dim,
            transcendentals=0,
        ),
    )(features, own, other)


def inward_kernel(rows_ref, w_in_ref, hidden_ref):
    depth = rows_ref.shape[1] // 2
    total = jnp.dot(rows_ref[:, :depth], w_in_ref[:depth, :], preferred_element_type=F32)
    hidden_ref[...] = total
    hidden_ref[...] += jnp.dot(rows_ref[:, depth:], w_in_ref[depth:, :], preferred_element_type=F32)


def inward(rows, w_in):
    count, model_dim = rows.shape
    hidden = w_in.shape[1]
    return pl.pallas_call(
        inward_kernel,
        in_specs=whole(2),
        out_specs=whole(1)[0],
        out_shape=pltpu.VMEM((count, hidden), F32),
        compiler_params=pltpu.CompilerParams(vmem_limit_bytes=6 << 20),
        cost_estimate=pl.CostEstimate(
            flops=2 * count * model_dim * hidden,
            bytes_accessed=2 * model_dim * hidden + 2 * count * model_dim,
            transcendentals=0,
        ),
    )(rows, w_in)


def middle_kernel(early_ref, rows_ref, order_ref, w_in_ref, w_out_ref, active_ref, *last_refs):
    late = jnp.dot(rows_ref[...], w_in_ref[...], preferred_element_type=F32)
    hidden = jnp.concatenate([early_ref[...], late], axis=0)
    active = (hidden * jax.nn.sigmoid(hidden)).astype(BF16)
    active = jnp.dot(order_ref[...], active, preferred_element_type=F32).astype(BF16)
    active_ref[...] = active
    write_blocks(active[early_ref.shape[0] :], w_out_ref, last_refs, 2)


def write_blocks(active, w_out_ref, refs, pieces):
    rows, model_dim = refs[0].shape
    piece = model_dim // pieces
    for i in range(pieces):
        at = slice(i * piece, (i + 1) * piece)
        result = jnp.dot(active, w_out_ref[:, at], preferred_element_type=F32)
        for j, ref in enumerate(refs):
            ref[:, at] = result[j * rows : (j + 1) * rows].astype(BF16)


def middle(early, rows, order, w_in, w_out, block):
    count, model_dim = rows.shape
    hidden = w_in.shape[1]
    total = early.shape[0] + count
    return pl.pallas_call(
        middle_kernel,
        in_specs=whole(5),
        out_specs=whole(1 + count // block),
        out_shape=[pltpu.VMEM((total, hidden), BF16)]
        + [pltpu.VMEM((block, model_dim), BF16)] * (count // block),
        compiler_params=pltpu.CompilerParams(vmem_limit_bytes=8 << 20),
        cost_estimate=pl.CostEstimate(
            flops=4 * count * model_dim * hidden,
            bytes_accessed=4 * model_dim * hidden,
            transcendentals=total * hidden,
        ),
    )(early, rows, order, w_in, w_out)


def outward_kernel(active_ref, w_out_ref, *out_refs):
    rows = len(out_refs) * out_refs[0].shape[0]
    write_blocks(active_ref[0:rows, :], w_out_ref, out_refs, 3)


def outward(active, w_out, blocks, block):
    hidden, model_dim = w_out.shape
    count = blocks * block
    return pl.pallas_call(
        outward_kernel,
        in_specs=whole(2),
        out_specs=whole(blocks),
        out_shape=[pltpu.VMEM((block, model_dim), BF16)] * blocks,
        compiler_params=pltpu.CompilerParams(vmem_limit_bytes=8 << 20),
        cost_estimate=pl.CostEstimate(
            flops=2 * count * model_dim * hidden,
            bytes_accessed=2 * model_dim * hidden + 2 * count * model_dim,
            transcendentals=0,
        ),
    )(active, w_out)


def gather_heads(own, w_in, w_out, aside):
    own, w_in = lax.optimization_barrier((own, w_in))
    from_down = send(own, Z_UP)
    from_up = send(own, Z_DOWN)
    far = send(own, Z_FAR)
    beside = send(own, Y_LO)
    w_in = stage(w_in)
    aside = send(aside, SWAP)
    beside, far, aside, w_out = lax.optimization_barrier((beside, far, aside, w_out))
    beside_down = send(beside, Z_UP)
    beside_up = send(beside, Z_DOWN)
    beside_far = send(far, Y_LO)
    w_out = stage(w_out)
    early = inward(jnp.concatenate([own, from_up, from_down, far, beside]), w_in)
    late = jnp.concatenate([beside_up, beside_down, beside_far])
    return early, late, w_in, w_out, aside


def sum_kernel(*refs):
    total = refs[0][...].astype(F32)
    for ref in refs[1:-1]:
        total = total + ref[...].astype(F32)
    refs[-1][...] = total.astype(BF16)


def add(*arrays):
    return pl.pallas_call(
        sum_kernel,
        in_specs=whole(len(arrays)),
        out_specs=whole(1)[0],
        out_shape=pltpu.VMEM(arrays[0].shape, BF16),
        compiler_params=pltpu.CompilerParams(vmem_limit_bytes=4 << 20),
    )(*arrays)


def last_sum_kernel(*refs):
    out_ref = refs[-1]
    total = refs[0][...].astype(F32)
    for ref in refs[1:-1]:
        total = total + ref[...].astype(F32)
    for i in range(out_ref.shape[0]):
        out_ref[i] = total[CAP * i : CAP * (i + 1)].astype(BF16)


def scatter_heads(own, up, down, far, beside, beside_up, beside_down, beside_far):
    rows, width = own.shape
    first = send(beside_up, Z_UP)
    second = send(beside_down, Z_DOWN)
    third = send(beside_far, Y_LO)
    from_far = send(add(far, third), Z_FAR)
    from_down = send(up, Z_UP)
    from_up = send(down, Z_DOWN)
    from_beside = send(add(beside, first, second), Y_LO)
    return pl.pallas_call(
        last_sum_kernel,
        in_specs=whole(5),
        out_specs=whole(1)[0],
        out_shape=pltpu.HBM((rows // CAP, CAP, width), BF16),
        compiler_params=pltpu.CompilerParams(vmem_limit_bytes=6 << 20),
        cost_estimate=pl.CostEstimate(
            flops=0, bytes_accessed=12 * rows * width, transcendentals=0
        ),
    )(own, from_down, from_up, from_far, from_beside)


def finish_kernel(returned_ref, resid_ref, weights_ref, out_ref):
    members, steps, width = out_ref.shape[1:]
    tokens = members * steps
    slots = weights_ref.shape[1]
    copies = returned_ref.shape[0] // slots
    piece = width // 4
    for i in range(4):
        at = slice(i * piece, (i + 1) * piece)
        total = returned_ref[0:slots, at].astype(F32)
        for copy in range(1, copies):
            total = total + returned_ref[copy * slots : (copy + 1) * slots, at].astype(F32)
        mixed = jnp.dot(weights_ref[...], total.astype(BF16), preferred_element_type=F32)
        mixed = mixed[:tokens] + mixed[tokens:]
        decoded = resid_ref[:, at].astype(F32) + mixed
        for member in range(members):
            out_ref[0, member, :, at] = decoded[member * steps : (member + 1) * steps].astype(BF16)


def finish(returned, resid, weights, members, steps, width):
    return pl.pallas_call(
        finish_kernel,
        in_specs=whole(3),
        out_specs=whole(1)[0],
        out_shape=jax.ShapeDtypeStruct((1, members, steps, width), BF16),
        compiler_params=pltpu.CompilerParams(vmem_limit_bytes=6 << 20),
    )(returned, resid, weights)


def on_device(
    k_pre,
    v_pre,
    pre_decay,
    q_dec,
    k_dec,
    v_dec,
    dec_decay,
    x_dec,
    route,
    att_gain,
    w_o,
    ffn_gain,
    w_router,
    w_in,
    w_out,
):
    head_id = lax.axis_index("head")
    n_head, n_exp = lax.axis_size("head"), lax.axis_size("exp")
    owned, steps, width = q_dec.shape[1:]
    tokens = owned * steps
    model_dim = x_dec.shape[3]

    w_o_other = send(w_o, CORE)

    packed = pack_decode(q_dec, k_dec, v_dec, dec_decay, n_head)
    packed = lax.all_to_all(packed, "head", split_axis=0, concat_axis=0, tiled=True)
    features = readout_features(
        k_pre, v_pre, jnp.transpose(pre_decay, (0, 1, 3, 2)), packed, att_gain[None]
    )

    ids = route.reshape(tokens, 2)
    carried = jnp.concatenate(
        [
            x_dec.reshape(tokens, model_dim),
            jnp.pad(ids.astype(BF16), ((0, 0), (0, EXTRA - 2))),
        ],
        axis=1,
    )
    features, carried, w_o_other = lax.optimization_barrier((features, carried, w_o_other))
    features = send(features, SWAP)
    carried = send(carried, SWAP)
    x_here = carried[:, :model_dim]
    ids_here = carried[:, model_dim : model_dim + 2].astype(jnp.int32)
    w_o_other = stage(w_o_other)
    partial_sum = project(features, w_o, w_o_other)
    partial_sum = partial_sum.reshape(n_head, tokens, model_dim + EXTRA)
    parts = lax.all_to_all(
        partial_sum,
        "exp",
        split_axis=0,
        concat_axis=0,
        tiled=True,
        axis_index_groups=[list(range(c, n_exp, 2)) for c in range(2)],
    )
    summed = jnp.sum(parts.astype(F32), axis=0)
    squares = summed[:, model_dim : model_dim + 1] + summed[:, model_dim + 1 : model_dim + 2]
    attn = summed[:, :model_dim] * lax.rsqrt(squares / width + 1e-06)
    resid = (x_here.astype(F32) + attn).astype(BF16)
    resid_f = resid.astype(F32)
    mean_square = jnp.mean(resid_f * resid_f, axis=-1, keepdims=True)
    ffn_in = (resid_f * lax.rsqrt(mean_square + 1e-06) * ffn_gain).astype(BF16)

    experts = w_router.shape[1]
    logits = jnp.dot(ffn_in, w_router, preferred_element_type=F32)

    def slots_of(expert_ids):
        flat_ids = expert_ids.reshape(-1)
        order = jnp.arange(flat_ids.shape[0], dtype=jnp.int32)
        earlier = (flat_ids[:, None] == flat_ids[None, :]) & (order[:, None] > order[None, :])
        slots = jnp.sum(earlier.astype(jnp.int32), axis=1)
        target = (flat_ids * CAP + slots).reshape(tokens, 2)
        places = jnp.arange(experts * CAP, dtype=jnp.int32)
        return places[None, None, :] == target[:, :, None]

    table = jnp.sum(slots_of(ids_here).astype(F32), axis=1).astype(BF16)
    rows = jnp.dot(table.T, ffn_in, preferred_element_type=F32).astype(BF16)
    rows = rows.reshape(n_exp, CAP, model_dim)
    onehot = (ids_here[:, :, None] == jnp.arange(experts, dtype=jnp.int32)).astype(F32)
    gates = jax.nn.sigmoid(jnp.sum(onehot * logits[:, None, :], axis=-1))
    weights = gates / jnp.sum(gates, axis=-1, keepdims=True)
    weight_parts = jnp.concatenate(split_two(weights), axis=1)

    rows = lax.all_to_all(rows, "exp", split_axis=0, concat_axis=0, tiled=True)
    back = jnp.concatenate([resid, jnp.pad(weight_parts, ((0, 0), (0, EXTRA - 4)))], axis=1)
    early, late, near_in, near_out, back = gather_heads(
        rows.reshape(n_exp * CAP, model_dim), w_in[0], w_out[0], back
    )

    count = n_head * n_exp * CAP
    per_group = count // n_head // n_head
    offsets = jnp.array([0, 2, 6, 4, 1, 3, 7, 5], jnp.int32)

    def position(relative):
        step = offsets[relative]
        return ((head_id // 2 + step // 2) % 4) * 2 + (head_id % 2 + step % 2) % 2

    leaving = jnp.arange(count, dtype=jnp.int32)
    block = n_head * per_group
    goes_to = position(leaving // block)
    came_from = (leaving % block) // per_group
    key_out = (came_from * n_head + goes_to) * per_group + leaving % per_group
    key_in = (position(leaving // block) * n_head + (leaving % block) // per_group) * per_group
    key_in = key_in + leaving % per_group
    order = (key_out[:, None] == key_in[None, :]).astype(BF16)
    active, *last = middle(early, late, order, near_in, near_out, block)
    outputs = scatter_heads(*outward(active, near_out, early.shape[0] // block, block), *last)
    returned = lax.all_to_all(
        outputs, "exp", split_axis=0, concat_axis=0, tiled=True
    ).reshape(n_exp * CAP, model_dim)

    weights_here = back[:, model_dim : model_dim + 2].astype(F32)
    weights_here = weights_here + back[:, model_dim + 2 : model_dim + 4].astype(F32)
    spread = jnp.sum(slots_of(ids).astype(F32) * weights_here[:, :, None], axis=1)
    spread = jnp.concatenate(split_two(spread), axis=0)
    return finish(returned, back, spread, owned, steps, model_dim)


def solution(mesh):
    return jax.shard_map(
        on_device,
        mesh=mesh,
        in_specs=(
            P(None, "exp", None, "head"),
            P(None, "exp", None, "head"),
            P(None, "exp", None, "head"),
            P("head", "exp", None, None),
            P("head", "exp", None, None),
            P("head", "exp", None, None),
            P("head", "exp", None, None),
            P("head", "exp", None, None),
            P("head", "exp", None, None),
            P(),
            P("exp", None),
            P(),
            P(),
            P("exp", None, "head"),
            P("exp", "head", None),
        ),
        out_specs=P("head", "exp", None, None),
        check_vma=False,
    )
```
